512 devices in a mesh: gx: 16 (over z), gy: 8 (over x, core), gz: 4 (over y).
Axes of the slice: x: 4, y: 4, z: 16, core: 2. Of those that a mesh axis runs over, the one named last changes fastest.
Arguments:
- box_counts: int32 [32], replicated, may hold values from 2 to 4, as said below
- viscosity: float32 [3], replicated, may hold values from 0.5 to 2
- implicit_coef: float32 [16, 128, 32, 512], P('gx', ('gy', 'gz')), may hold values from 0.02 to 0.5
- right_side: float32 [16, 128, 3, 32, 512], P('gx', ('gy', 'gz')), may hold values from -8 to 8
- old_direction: float32 [16, 128, 3, 32, 512], P('gx', ('gy', 'gz')), may hold values from -6 to 6
- previous_dot: float32 [1], replicated, may hold values from 0.05 to 0.5
Outputs:
- smoothed: float32 [16, 128, 3, 32, 512], P('gx', ('gy', 'gz'))
- direction: float32 [16, 128, 3, 32, 512], P('gx', ('gy', 'gz'))
The draws below stay inside these ranges and needn't reach their ends.
Inputs may be any that keep to these rules, and one draw needn't show every extreme that they name: `box_counts`: every device holds from 2 to 4 columns; in every draw one device holds exactly 4 and another exactly 2; the total is even.
All inputs are finite; a program needn't handle non-finite values.
Results may differ from the reference program's by a relative error of at most 0.00005.
Values sent between devices are 32-bit elements; how exact they have to be, the bound alone decides.
No kernel may reach another device: no remote copies, remote signals or barrier semaphores. Data moves between devices by JAX's collectives and lax.ppermute only.
A program may use at most 64 MiB of HBM per device.

```python
import math
import jax
import jax.numpy as jnp

EDGE = 16
SLOTS = 4
SWEEPS_FINE = 2
SWEEPS_COARSE = 4
GROUP = 32
NSLAB = 16


def draw_box_counts(key, part):
    key = jax.random.fold_in(key, 7)
    first_key, second_key = jax.random.split(key)
    drawn = jax.random.randint(first_key, (GROUP,), 2, SLOTS + 1).astype(jnp.int32)
    order = jax.random.permutation(second_key, GROUP - 1)
    places = jnp.arange(GROUP, dtype=jnp.int32)
    drawn = jnp.where(places == order[0], SLOTS, drawn)
    drawn = jnp.where(places == order[1], 2, drawn)
    last_one = drawn[GROUP - 1]
    parity_bit = jnp.sum(drawn) % 2
    mended = jnp.where(parity_bit == 1, jnp.where(last_one == SLOTS, last_one - 1, last_one + 1), last_one)
    return jnp.where(places == GROUP - 1, mended, drawn).astype(jnp.int32)


def draw_right_side(key, part):
    key = jax.random.fold_in(key, 11)
    rows_all = GROUP * SLOTS
    shape = (NSLAB, rows_all, 3, 2 * EDGE, 2 * EDGE * EDGE)
    slab_pos = jnp.arange(NSLAB, dtype=jnp.float32) / max(NSLAB - 1, 1)
    row_pos = jnp.arange(rows_all, dtype=jnp.float32) / (rows_all - 1)
    scale = (0.5 * (1.0 + slab_pos)[:, None] * (1.0 + row_pos)[None, :])[:, :, None, None, None]
    base = jnp.clip(jax.random.normal(key, shape, jnp.float32), -4.0, 4.0)
    return base * scale


def block_scale(key, extent, shards, smallest, largest):
    loudness, own = 1.0, jax.random.fold_in(key, 6)
    for dim, parts in shards:
        heights = jnp.exp(jax.random.uniform(jax.random.fold_in(own, dim), (parts,), jnp.float32, smallest / len(shards), largest / len(shards)))
        loudness = loudness * jnp.repeat(heights, extent[dim] // parts).reshape([-1 if axis == dim else 1 for axis in range(len(extent))])
    return loudness


def centred(stream_key, dims, spread, reach, pieces=(), kind=jnp.bfloat16):
    factor_of = block_scale(stream_key, dims, pieces, -0.22, 0.18) if pieces else 1.0
    values = jax.random.normal(stream_key, dims, jnp.float32) * spread * factor_of
    return jnp.minimum(jnp.maximum(values, -reach), reach).astype(kind)


def setup_inputs(seed: int = 0) -> dict:
    keys = jax.random.split(jax.random.key(seed), 7)
    return {
        "box_counts": draw_box_counts(jax.random.fold_in(keys[6], 71), 0),
        "viscosity": jnp.clip(jnp.exp(jax.random.uniform(keys[1], (3,), jnp.float32, math.log(0.5), math.log(2.0))), 0.5, 2.0),
        "implicit_coef": jnp.clip(jnp.exp(math.log(0.5) - 3.218876 * jax.random.uniform(keys[2], (NSLAB, GROUP * SLOTS, 2 * EDGE, 2 * EDGE * EDGE), jnp.float32) ** block_scale(keys[2], (NSLAB, GROUP * SLOTS, 2 * EDGE, 2 * EDGE * EDGE), ((0, 16), (1, 32)), -0.2, 0.2)), 0.02, 0.5),
        "right_side": draw_right_side(jax.random.fold_in(keys[6], 71), 0),
        "old_direction": centred(keys[4], (NSLAB, GROUP * SLOTS, 3, 2 * EDGE, 2 * EDGE * EDGE), 1.0, 6.0, ((0, 16), (1, 32)), jnp.float32),
        "previous_dot": jnp.clip(jnp.exp(jax.random.uniform(keys[5], (1,), jnp.float32, math.log(0.05), math.log(0.5))), 0.05, 0.5),
    }


def neighbor_total(values):
    padded = jnp.pad(values, ((0, 0), (1, 1), (1, 1), (1, 1)))
    total_sum = padded[:, 2:, 1:-1, 1:-1] + padded[:, :-2, 1:-1, 1:-1]
    total_sum = total_sum + padded[:, 1:-1, 2:, 1:-1] + padded[:, 1:-1, :-2, 1:-1]
    return total_sum + padded[:, 1:-1, 1:-1, 2:] + padded[:, 1:-1, 1:-1, :-2]


def sweep_colour(values, source, diagonal, factor, chosen):
    updated = (source + factor * neighbor_total(values)) / diagonal
    return jnp.where(chosen, updated, values)


def parity(depth_n, cols_n, rows_n):
    summed = jnp.arange(depth_n, dtype=jnp.int32)[:, None, None] + jnp.arange(cols_n, dtype=jnp.int32)[None, :, None]
    return (summed + jnp.arange(rows_n, dtype=jnp.int32)[None, None, :]) % 2


def shrink(values):
    channels, depth_n, cols_n, rows_n = values.shape
    blocks = values.reshape(channels, depth_n // 2, 2, cols_n // 2, 2, rows_n // 2, 2)
    return jnp.sum(blocks, axis=(2, 4, 6)) * 0.125


def expand(values):
    return jnp.repeat(jnp.repeat(jnp.repeat(values, 2, axis=1), 2, axis=2), 2, axis=3)


def layout(box_counts):
    starts = (jnp.cumsum(box_counts) - box_counts).astype(jnp.int32)
    total_cols = jnp.sum(box_counts).astype(jnp.int32)
    return starts, total_cols


def to_dense(slotted, starts, total_cols):
    columns = jnp.arange(GROUP * SLOTS, dtype=jnp.int32)
    owner_dev = (jnp.sum((starts[None, :] <= columns[:, None]).astype(jnp.int32), axis=1) - 1).astype(jnp.int32)
    slot_of = owner_dev * SLOTS + columns - jnp.take(starts, owner_dev)
    live_col = columns < total_cols
    slot_of = jnp.where(live_col, slot_of, 0).astype(jnp.int32)
    picked = jnp.take(slotted, slot_of, axis=1)
    picked = jnp.where(live_col[None, :, None, None, None], picked, 0.0)
    nslab_n, ncol_n, channels, depth_n, flat_n = picked.shape
    picked = picked.reshape(nslab_n, ncol_n, channels, depth_n, EDGE, flat_n // EDGE)
    return picked.transpose(2, 0, 3, 1, 4, 5).reshape(channels, nslab_n * depth_n, ncol_n * EDGE, flat_n // EDGE)


def to_slots(dense, starts, box_counts):
    channels, depth_all, cols_all, rows_n = dense.shape
    ncol_n = cols_all // EDGE
    depth_n = 2 * EDGE
    blocks = dense.reshape(channels, depth_all // depth_n, depth_n, ncol_n, EDGE, rows_n)
    blocks = blocks.transpose(1, 3, 0, 2, 4, 5).reshape(depth_all // depth_n, ncol_n, channels, depth_n, EDGE * rows_n)
    slot_ids = jnp.arange(GROUP * SLOTS, dtype=jnp.int32)
    owner_dev = slot_ids // SLOTS
    place = slot_ids % SLOTS
    column_of = (jnp.take(starts, owner_dev) + place).astype(jnp.int32)
    keep = place < jnp.take(box_counts, owner_dev)
    picked = jnp.take(blocks, jnp.clip(column_of, 0, ncol_n - 1), axis=1)
    keep_mask = keep[None, :, None, None, None]
    return jnp.where(keep_mask, picked, 0.0), keep_mask


def reference(box_counts, viscosity, implicit_coef, right_side, old_direction, previous_dot):
    starts, total_cols = layout(box_counts)
    source = to_dense(right_side, starts, total_cols)
    coef_dense = to_dense(implicit_coef[:, :, None], starts, total_cols)[0]
    depth_n, cols_n, rows_n = coef_dense.shape
    live_x = (jnp.arange(cols_n, dtype=jnp.int32) < total_cols * EDGE)[None, :, None]
    factor = viscosity[:, None, None, None]
    diagonal = coef_dense[None] + 6.0 * factor
    colours = parity(depth_n, cols_n, rows_n)
    red_cells = live_x & (colours == 0)
    black_cells = live_x & (colours == 1)
    values = jnp.zeros_like(source)
    for sweep_no in range(SWEEPS_FINE):
        values = sweep_colour(values, source, diagonal, factor, red_cells)
        values = sweep_colour(values, source, diagonal, factor, black_cells)
    remain = jnp.where(live_x, source - (diagonal * values - factor * neighbor_total(values)), 0.0)
    coarse_source = shrink(remain)
    coarse_coef = shrink(coef_dense[None])[0]
    coarse_factor = factor * 0.25
    coarse_diag = coarse_coef[None] + 6.0 * coarse_factor
    live_coarse = (jnp.arange(cols_n // 2, dtype=jnp.int32) < total_cols * (EDGE // 2))[None, :, None]
    coarse_colours = parity(depth_n // 2, cols_n // 2, rows_n // 2)
    coarse_red = live_coarse & (coarse_colours == 0)
    coarse_black = live_coarse & (coarse_colours == 1)
    correction = jnp.zeros_like(coarse_source)
    for sweep_no in range(SWEEPS_COARSE):
        correction = sweep_colour(correction, coarse_source, coarse_diag, coarse_factor, coarse_red)
        correction = sweep_colour(correction, coarse_source, coarse_diag, coarse_factor, coarse_black)
    values = values + jnp.where(live_x, expand(correction), 0.0)
    for sweep_no in range(SWEEPS_FINE):
        values = sweep_colour(values, source, diagonal, factor, black_cells)
        values = sweep_colour(values, source, diagonal, factor, red_cells)
    cell_total = total_cols.astype(jnp.float32) * (3.0 * depth_n * rows_n * EDGE)
    dot_mean = jnp.sum(source * values) / cell_total
    ratio = dot_mean / previous_dot[0]
    smoothed, keep_mask = to_slots(values, starts, box_counts)
    direction = jnp.where(keep_mask, smoothed + ratio * old_direction, 0.0)
    return smoothed, direction
```

```python
import functools

import jax
import jax.numpy as jnp
from jax import lax
from jax.experimental import pallas as pl
from jax.experimental.pallas import tpu as pltpu
from jax.sharding import PartitionSpec as P

GROUP_AXES = ("gy", "gz")
F32 = jnp.float32
BF16 = jnp.bfloat16
VMEM_BYTES = 48 * 1024 * 1024

SLOTS = 4
TILES = 2 * SLOTS
ROWS = 48
WIDE = TILES + 4
COWN = 16
CHALO = 10
CROWS = COWN + 2 * CHALO
CWIDE = SLOTS + 6


def iota(shape, dim):
    return lax.broadcasted_iota(jnp.int32, shape, dim)


def exact_dot(values, ones):
    high = values.astype(BF16)
    rest = values - high.astype(F32)
    mid = rest.astype(BF16)
    low = (rest - mid.astype(F32)).astype(BF16)
    total = jnp.dot(low, ones, preferred_element_type=F32)
    total = total + jnp.dot(mid, ones, preferred_element_type=F32)
    return total + jnp.dot(high, ones, preferred_element_type=F32)


def split_matrix():
    source, target = iota((256, 256), 0), iota((256, 256), 1)
    y = source % 32
    wanted = (y % 2) * 128 + source // 32 * 16 + y // 2
    return (target == wanted).astype(F32).astype(BF16)


def merge_matrix():
    source, target = iota((256, 256), 0), iota((256, 256), 1)
    y = target % 32
    wanted = (y % 2) * 128 + target // 32 * 16 + y // 2
    return (source == wanted).astype(F32).astype(BF16)


def pool_matrix():
    source, target = iota((256, 128), 0), iota((256, 128), 1)
    wanted = source // 32 * 16 + source % 16
    return (target == wanted).astype(F32).astype(BF16)


def spread_matrix():
    source, target = iota((128, 256), 0), iota((128, 256), 1)
    wanted = target // 32 * 16 + target % 16
    return (source == wanted).astype(F32).astype(BF16)


def even_cells(rows):
    shape = (rows, 128)
    return (iota(shape, 0) + iota(shape, 1) // 16) % 2 == 0


def pack_kernel(count, right, coef, above, below, packed, left_edge, right_edge):
    slot = pl.program_id(0)
    live = slot < count[0]
    split = split_matrix()
    even = even_cells(4 * ROWS)
    for half in range(2):
        lanes = slice(256 * half, 256 * half + 256)
        parts = []
        for m in range(4):
            own = right[0, m, :, lanes] if m < 3 else coef[0, :, lanes]
            parts += [above[0, m, :, lanes], own, below[0, m, :, lanes]]
        cells = jnp.where(live, jnp.concatenate(parts, axis=0), 0.0)
        both = exact_dot(cells, split)
        first, second = both[:, :128], both[:, 128:]
        red = jnp.where(even, first, second)
        black = jnp.where(even, second, first)
        for m in range(4):
            rows = slice(ROWS * m, ROWS * m + ROWS)
            packed[m, 0, half] = red[rows]
            packed[m, 1, half] = black[rows]

    @pl.when(slot == 0)
    def _():
        left_edge[...] = packed[:, :, 0]

    @pl.when(slot == count[0] - 1)
    def _():
        right_edge[...] = packed[:, :, 1]


def load_fine(count, factor, packed, from_left, from_right, scaled, ratio):
    def put(tile, take):
        out = []
        for colour in range(2):
            coef = take(3, colour)
            inside = coef > 0.0
            for m in range(3):
                inverse = jnp.where(inside, 1.0 / (coef + 6.0 * factor[m]), 0.0)
                out.append((m, colour, take(m, colour) * inverse, factor[m] * inverse))
        for m, colour, first, second in out:
            scaled[m, colour, tile] = first
            ratio[m, colour, tile] = second

    def own(tile, carry):
        put(tile + 2, lambda m, colour: packed[m, colour, tile])
        return carry

    lax.fori_loop(0, TILES, own, 0)
    put(1, lambda m, colour: from_left[m, colour])
    none = jnp.zeros((3, 2, ROWS, 128), F32)
    for tile in (0, WIDE - 2, WIDE - 1):
        scaled[:, :, tile] = none
        ratio[:, :, tile] = none
    put(2 * count + 2, lambda m, colour: from_right[m, colour])


def fine_update(other, scaled, ratio, m, colour, tile, chunk, masks):
    lane_low, lane_high, even, edges = masks
    row = 8 + 8 * chunk
    here = other[m, tile, row : row + 8]
    total = here + other[m, tile, row - 1 : row + 7]
    total = total + other[m, tile, row + 1 : row + 9]
    before = other[m, tile - 1, row : row + 8]
    after = other[m, tile + 1, row : row + 8]
    total = total + pltpu.roll(jnp.where(lane_high, before, here), 16, 1)
    total = total + pltpu.roll(jnp.where(lane_low, after, here), 112, 1)
    up, down = pltpu.roll(here, 1, 1), pltpu.roll(here, 127, 1)
    beside = jnp.where(even, up, down) if colour == 0 else jnp.where(even, down, up)
    total = total + jnp.where(edges[colour], 0.0, beside)
    rows = slice(8 * chunk, 8 * chunk + 8)
    return scaled[m, colour, tile, rows] + ratio[m, colour, tile, rows] * total


def fine_masks():
    lane = iota((8, 128), 1)
    even = even_cells(8)
    first, last = lane % 16 == 0, lane % 16 == 15
    edges = (
        (even & first) | (jnp.logical_not(even) & last),
        (even & last) | (jnp.logical_not(even) & first),
    )
    return lane < 16, lane >= 112, even, edges


def fine_sweep(values, scaled, ratio, colour, masks):
    def body(tile, carry):
        found = [
            (m, chunk, fine_update(values[1 - colour], scaled, ratio, m, colour, tile, chunk, masks))
            for m in range(3)
            for chunk in range(ROWS // 8)
        ]
        for m, chunk, new in found:
            values[colour][m, tile, 8 + 8 * chunk : 16 + 8 * chunk] = new
        return carry

    lax.fori_loop(1, WIDE - 1, body, 0, unroll=2)


def down_kernel(
    count, factor, packed, from_left, from_right, red, black, coarse, to_above, to_below, partial,
    scaled, ratio, remain
):
    held = count[0]
    load_fine(held, factor, packed, from_left, from_right, scaled, ratio)
    masks = fine_masks()
    pre = (red, black)
    red[...] = jnp.zeros(red.shape, F32)
    black[...] = jnp.zeros(black.shape, F32)
    red[:, :, 8 : 8 + ROWS] = scaled[:, 0]
    fine_sweep(pre, scaled, ratio, 1, masks)
    fine_sweep(pre, scaled, ratio, 0, masks)
    fine_sweep(pre, scaled, ratio, 1, masks)

    def residual(tile, total):
        found = []
        for chunk in range(1, 5):
            rows = slice(8 * chunk, 8 * chunk + 8)
            row = 8 + 8 * chunk
            coef = packed[3, 0, tile - 2, rows]
            out = slice(8 * chunk - 8, 8 * chunk)
            for m in range(3):
                reds = red[m, tile, row : row + 8]
                blacks = black[m, tile, row : row + 8]
                update = fine_update(black, scaled, ratio, m, 0, tile, chunk, masks)
                left = (coef + 6.0 * factor[m]) * (update - reds)
                left = jnp.where(tile < 2 * held + 2, left, 0.0)
                found.append((m, out, left))
                term = (packed[m, 0, tile - 2, rows] + left) * reds
                total = total + term + packed[m, 1, tile - 2, rows] * blacks
            found.append((3, out, coef + packed[3, 1, tile - 2, rows]))
        for m, out, left in found:
            remain[m, tile - 2, out] = left
        return total

    total = lax.fori_loop(2, 2 + TILES, residual, jnp.zeros((8, 128), F32))
    partial[...] = total
    pool = pool_matrix()
    for slot in range(SLOTS):
        sides = []
        for tile in (2 * slot, 2 * slot + 1):
            sides.append(
                jnp.concatenate(
                    [
                        remain[m, tile, pl.ds(0, COWN, stride=2)]
                        + remain[m, tile, pl.ds(1, COWN, stride=2)]
                        for m in range(4)
                    ],
                    axis=0,
                )
            )
        pooled = exact_dot(jnp.concatenate(sides, axis=1), pool) * 0.125
        for m in range(4):
            box = pooled[COWN * m : COWN * m + COWN]
            coarse[m, slot] = box
            to_above[m, CHALO * slot : CHALO * slot + CHALO] = box[:CHALO]
            to_below[m, CHALO * slot : CHALO * slot + CHALO] = box[COWN - CHALO :]


def up_kernel(
    count, factor, packed, from_left, from_right, pre_red, pre_black, coarse, above, below,
    coarse_left, coarse_right, partial, smoothed, share, scaled, ratio, red, black, cscaled,
    cratio, cred, cblack, spread
):
    held = count[0]
    cscaled[...] = jnp.zeros(cscaled.shape, F32)
    cratio[...] = jnp.zeros(cratio.shape, F32)

    def put(tile, row, pieces):
        coef = pieces[3]
        size = coef.shape[0]
        for m in range(3):
            b = 0.25 * factor[m]
            inverse = jnp.where(coef > 0.0, 1.0 / (coef + 6.0 * b), 0.0)
            cscaled[m, tile, row : row + size] = pieces[m] * inverse
            cratio[m, tile, row : row + size] = b * inverse

    for slot in range(SLOTS):
        rows = slice(CHALO * slot, CHALO * slot + CHALO)
        put(slot + 3, 0, [above[m, rows] for m in range(4)])
        put(slot + 3, CHALO, [coarse[m, slot] for m in range(4)])
        put(slot + 3, CHALO + COWN, [below[m, rows] for m in range(4)])
    for side in range(2):
        rows = slice(CROWS * side, CROWS * side + CROWS)
        put(1 + side, 0, [coarse_left[m, rows] for m in range(4)])
        put(held + 3 + side, 0, [coarse_right[m, rows] for m in range(4)])

    lane = iota((8, 128), 1)
    lane_low, lane_high = lane < 16, lane >= 112
    first, last = lane % 16 == 0, lane % 16 == 15
    is_red = (iota((8, 128), 0) + lane // 16 + lane % 16) % 2 == 0
    chosen = (is_red, jnp.logical_not(is_red))
    corr = (cred, cblack)
    cred[...] = jnp.zeros(cred.shape, F32)
    cblack[...] = jnp.zeros(cblack.shape, F32)

    def start(tile, carry):
        found = [
            (m, chunk, jnp.where(is_red, cscaled[m, tile, 8 * chunk : 8 * chunk + 8], 0.0))
            for m in range(3)
            for chunk in range(5)
        ]
        for m, chunk, new in found:
            cred[m, tile, 8 + 8 * chunk : 16 + 8 * chunk] = new
        return carry

    lax.fori_loop(1, CWIDE - 1, start, 0)

    def coarse_sweep(colour):
        other = corr[1 - colour]

        def body(tile, carry):
            found = []
            for m in range(3):
                for chunk in range(5):
                    row = 8 + 8 * chunk
                    here = other[m, tile, row : row + 8]
                    total = other[m, tile, row - 1 : row + 7] + other[m, tile, row + 1 : row + 9]
                    before = other[m, tile - 1, row : row + 8]
                    after = other[m, tile + 1, row : row + 8]
                    total = total + pltpu.roll(jnp.where(lane_high, before, here), 16, 1)
                    total = total + pltpu.roll(jnp.where(lane_low, after, here), 112, 1)
                    total = total + jnp.where(first, 0.0, pltpu.roll(here, 1, 1))
                    total = total + jnp.where(last, 0.0, pltpu.roll(here, 127, 1))
                    rows = slice(8 * chunk, 8 * chunk + 8)
                    new = cscaled[m, tile, rows] + cratio[m, tile, rows] * total
                    found.append((m, row, jnp.where(chosen[colour], new, 0.0)))
            for m, row, new in found:
                corr[colour][m, tile, row : row + 8] = new
            return carry

        lax.fori_loop(1, CWIDE - 1, body, 0, unroll=2)

    coarse_sweep(1)
    for _ in range(3):
        coarse_sweep(0)
        coarse_sweep(1)

    total = partial[...]
    for slot in range(SLOTS):
        for m in range(3):
            for chunk in range(2):
                row = 8 + CHALO + 8 * chunk
                both = cred[m, slot + 3, row : row + 8] + cblack[m, slot + 3, row : row + 8]
                total = total + 8.0 * (coarse[m, slot, 8 * chunk : 8 * chunk + 8] * both)
    share[...] = jnp.broadcast_to(jnp.sum(total, axis=0, keepdims=True), share.shape)

    load_fine(held, factor, packed, from_left, from_right, scaled, ratio)
    masks = fine_masks()
    values = (red, black)
    for value in values:
        value[...] = jnp.zeros(value.shape, F32)
    widen = spread_matrix()
    half_rows = ROWS // 2
    for ctile in range(2, CWIDE - 2):
        low = 8 + CHALO - 4
        cells = jnp.concatenate(
            [
                cred[m, ctile, low : low + half_rows] + cblack[m, ctile, low : low + half_rows]
                for m in range(3)
            ],
            axis=0,
        )
        wide = exact_dot(cells, widen)
        for half in range(2):
            tile = 2 * (ctile - 3) + half + 2
            if not 1 <= tile <= WIDE - 2:
                continue
            for m in range(3):
                piece = wide[half_rows * m : half_rows * m + half_rows, 128 * half : 128 * half + 128]
                spread[m, tile, pl.ds(0, half_rows, stride=2)] = piece
                spread[m, tile, pl.ds(1, half_rows, stride=2)] = piece

    def add(tile, carry):
        found = [
            (value, m, old[m, tile, 8 : 8 + ROWS] + spread[m, tile])
            for value, old in ((red, pre_red), (black, pre_black))
            for m in range(3)
        ]
        for value, m, new in found:
            value[m, tile, 8 : 8 + ROWS] = new
        return carry

    lax.fori_loop(1, WIDE - 1, add, 0)
    for _ in range(2):
        fine_sweep(values, scaled, ratio, 1, masks)
        fine_sweep(values, scaled, ratio, 0, masks)

    merge = merge_matrix()
    even = even_cells(3 * 32)
    for slot in range(SLOTS):
        live = slot < held
        for half in range(2):
            tile = 2 + 2 * slot + half
            reds = jnp.concatenate([red[m, tile, 16:48] for m in range(3)], axis=0)
            blacks = jnp.concatenate([black[m, tile, 16:48] for m in range(3)], axis=0)
            both = jnp.concatenate(
                [jnp.where(even, reds, blacks), jnp.where(even, blacks, reds)], axis=1
            )
            cells = exact_dot(jnp.where(live, both, 0.0), merge)
            for m in range(3):
                smoothed[slot, m, :, 256 * half : 256 * half + 256] = cells[32 * m : 32 * m + 32]


def shape(*dims):
    return jax.ShapeDtypeStruct(dims, F32)


SMEM = pl.BlockSpec(memory_space=pltpu.SMEM)
WHOLE = pl.BlockSpec(memory_space=pltpu.VMEM)


def shift(value, axis, step):
    size = lax.axis_size(axis)
    pairs = [(i, i + step) for i in range(size) if 0 <= i + step < size]
    return lax.ppermute(value, axis, pairs)


def total_over(rows, axis):
    return jnp.sum(lax.all_to_all(rows, axis, 0, 0), axis=0)


def per_device(box_counts, viscosity, implicit_coef, right_side, old_direction, previous_dot):
    group_n = lax.axis_size(GROUP_AXES)
    slab_n = lax.axis_size("gx")
    my_index = lax.axis_index(GROUP_AXES)
    held = lax.dynamic_index_in_dim(box_counts, my_index, 0, keepdims=False)
    count = held[None]
    right, coef = right_side[0], implicit_coef[0]
    params = pltpu.CompilerParams(vmem_limit_bytes=VMEM_BYTES)

    top = jnp.concatenate([right[:, :, :8], coef[:, None, :8]], axis=1)
    bottom = jnp.concatenate([right[:, :, 24:], coef[:, None, 24:]], axis=1)
    above = shift(bottom, "gx", 1)
    below = shift(top, "gx", -1)

    slot_block = lambda *dims: pl.BlockSpec((1,) + dims, lambda q: (q,) + (0,) * len(dims))
    edge_block = pl.BlockSpec((4, 2, ROWS, 128), lambda q: (0, 0, 0, 0))
    packed, left_edge, right_edge = pl.pallas_call(
        pack_kernel,
        grid=(SLOTS,),
        in_specs=[
            SMEM,
            slot_block(3, 32, 512),
            slot_block(32, 512),
            slot_block(4, 8, 512),
            slot_block(4, 8, 512),
        ],
        out_specs=[
            pl.BlockSpec((4, 2, 2, ROWS, 128), lambda q: (0, 0, q, 0, 0)),
            edge_block,
            edge_block,
        ],
        out_shape=[
            shape(4, 2, TILES, ROWS, 128),
            shape(4, 2, ROWS, 128),
            shape(4, 2, ROWS, 128),
        ],
        compiler_params=params,
        name="pack",
    )(count, right, coef, above, below)

    from_left = shift(right_edge, GROUP_AXES, 1)
    from_right = shift(left_edge, GROUP_AXES, -1)

    padded = (3, WIDE, ROWS + 16, 128)
    fine = pltpu.VMEM((3, 2, WIDE, ROWS, 128), F32)
    pre_red, pre_black, coarse, to_above, to_below, partial = pl.pallas_call(
        down_kernel,
        in_specs=[SMEM, SMEM, WHOLE, WHOLE, WHOLE],
        out_specs=[WHOLE] * 6,
        out_shape=[
            shape(*padded),
            shape(*padded),
            shape(4, SLOTS, COWN, 128),
            shape(4, SLOTS * CHALO, 128),
            shape(4, SLOTS * CHALO, 128),
            shape(8, 128),
        ],
        scratch_shapes=[fine, fine, pltpu.VMEM((4, TILES, 32, 128), F32)],
        compiler_params=params,
        name="down",
    )(count, viscosity, packed, from_left, from_right)

    coarse_above = shift(to_below, "gx", 1)
    coarse_below = shift(to_above, "gx", -1)
    tall = jnp.concatenate(
        [
            coarse_above.reshape(4, SLOTS, CHALO, 128),
            coarse,
            coarse_below.reshape(4, SLOTS, CHALO, 128),
        ],
        axis=2,
    )
    edge_shape = (4, 2 * CROWS, 128)
    coarse_first = tall[:, :2].reshape(edge_shape)
    coarse_last = lax.dynamic_slice_in_dim(tall, held - 2, 2, axis=1).reshape(edge_shape)
    coarse_left = shift(coarse_last, GROUP_AXES, 1)
    coarse_right = shift(coarse_first, GROUP_AXES, -1)

    cfine = pltpu.VMEM((3, CWIDE, 40, 128), F32)
    smoothed, share = pl.pallas_call(
        up_kernel,
        in_specs=[SMEM, SMEM] + [WHOLE] * 11,
        out_specs=[WHOLE] * 2,
        out_shape=[shape(SLOTS, 3, 32, 512), shape(group_n, 128)],
        scratch_shapes=[
            fine,
            fine,
            pltpu.VMEM(padded, F32),
            pltpu.VMEM(padded, F32),
            cfine,
            cfine,
            pltpu.VMEM((3, CWIDE, 56, 128), F32),
            pltpu.VMEM((3, CWIDE, 56, 128), F32),
            pltpu.VMEM((3, WIDE, ROWS, 128), F32),
        ],
        compiler_params=params,
        name="up",
    )(
        count, viscosity, packed, from_left, from_right, pre_red, pre_black, coarse, coarse_above,
        coarse_below, coarse_left, coarse_right, partial
    )

    row = total_over(share, GROUP_AXES)
    row = total_over(jnp.broadcast_to(row[None], (slab_n, 128)), "gx")
    dot_total = jnp.sum(row)
    cell_total = jnp.sum(box_counts).astype(F32) * (3.0 * slab_n * 32 * 512)
    ratio = dot_total / cell_total / previous_dot[0]
    usable = (jnp.arange(SLOTS, dtype=jnp.int32) < held)[:, None, None, None]
    direction = jnp.where(usable, smoothed + ratio * old_direction[0], 0.0)
    return smoothed[None], direction[None]


def solution(mesh):
    wide = P("gx", GROUP_AXES, None, None, None)
    placed = (P(), P(), P("gx", GROUP_AXES, None, None), wide, wide, P())
    return jax.shard_map(
        per_device, mesh=mesh, in_specs=placed, out_specs=(wide, wide), check_vma=False
    )
```

```python
import functools

import jax
import jax.numpy as jnp
from jax import lax
from jax.experimental import pallas as pl
from jax.experimental.pallas import tpu as pltpu
from jax.sharding import PartitionSpec as P

GROUP_AXES = ("gy", "gz")
SLAB_AXIS = "gx"
F32 = jnp.float32
BF16 = jnp.bfloat16
VMEM_BYTES = 12 * 1024 * 1024

SLOTS = 4
TILES = 2 * SLOTS
ROWS = 48
NARROW = 40
WIDE = TILES + 4
COWN = 16
CHALO = 10
CROWS = COWN + 2 * CHALO
CWIDE = SLOTS + 6


def iota(shape, dim):
    return lax.broadcasted_iota(jnp.int32, shape, dim)


def exact_dot(values, ones):
    high = values.astype(BF16)
    rest = values - high.astype(F32)
    mid = rest.astype(BF16)
    low = (rest - mid.astype(F32)).astype(BF16)
    total = jnp.dot(low, ones, preferred_element_type=F32)
    total = total + jnp.dot(mid, ones, preferred_element_type=F32)
    return total + jnp.dot(high, ones, preferred_element_type=F32)


def split_matrix():
    source, target = iota((256, 256), 0), iota((256, 256), 1)
    y = source % 32
    wanted = (y % 2) * 128 + source // 32 * 16 + y // 2
    return (target == wanted).astype(F32).astype(BF16)


def merge_matrix():
    source, target = iota((256, 256), 0), iota((256, 256), 1)
    y = target % 32
    wanted = (y % 2) * 128 + target // 32 * 16 + y // 2
    return (source == wanted).astype(F32).astype(BF16)


def pool_matrix():
    source, target = iota((256, 128), 0), iota((256, 128), 1)
    wanted = source // 32 * 16 + source % 16
    return (target == wanted).astype(F32).astype(BF16)


def spread_matrix():
    source, target = iota((128, 256), 0), iota((128, 256), 1)
    wanted = target // 32 * 16 + target % 16
    return (source == wanted).astype(F32).astype(BF16)


def even_cells(rows):
    shape = (rows, 128)
    return (iota(shape, 0) + iota(shape, 1) // 16) % 2 == 0


def swap(value, axis, offset):
    size = lax.axis_size(axis)
    pairs = []
    for i in range(offset, size - 1, 2):
        pairs += [(i, i + 1), (i + 1, i)]
    return lax.ppermute(value, axis, pairs)


def exchange(first, second, axis):
    return swap(first, axis, 0), swap(second, axis, 1)


def split_cells(cells, rows, packed, put):
    even = even_cells(4 * rows)
    both = exact_dot(cells, packed)
    first, second = both[:, :128], both[:, 128:]
    red = jnp.where(even, first, second)
    black = jnp.where(even, second, first)
    for m in range(4):
        put(m, 0, red[rows * m : rows * m + rows])
        put(m, 1, black[rows * m : rows * m + rows])


def pack_kernel(info, right, coef, packed):
    live = pl.program_id(0) < info[0]
    split = split_matrix()
    for half in range(2):
        lanes = slice(256 * half, 256 * half + 256)
        parts = [right[0, m, :, lanes] for m in range(3)] + [coef[0, :, lanes]]
        cells = jnp.where(live, jnp.concatenate(parts, axis=0), 0.0)

        def put(m, colour, value, half=half):
            packed[m, colour, half] = value

        split_cells(cells, 32, split, put)


def pack_rim_kernel(info, above, below, rim):
    held = info[0]
    split = split_matrix()
    for slot in range(SLOTS):
        for half in range(2):
            lanes = slice(256 * half, 256 * half + 256)
            parts = []
            for m in range(4):
                parts += [above[slot, m, :, lanes], below[slot, m, :, lanes]]
            cells = jnp.where(slot < held, jnp.concatenate(parts, axis=0), 0.0)

            def put(m, colour, value, tile=2 * slot + half):
                rim[m, colour, tile] = value

            split_cells(cells, 16, split, put)


def pack_edges_kernel(info, above, below, packed, edge_a, edge_b):
    held, odd = info[0], info[2] == 1
    split = split_matrix()
    for slot, half in ((0, 0), (held - 1, 1)):
        lanes = slice(256 * half, 256 * half + 256)
        parts = []
        for m in range(4):
            parts += [above[slot, m, :, lanes], below[slot, m, :, lanes]]
        found = {}

        def put(m, colour, value):
            found[m, colour] = value

        split_cells(jnp.concatenate(parts, axis=0), 16, split, put)
        tile = 2 * slot + half
        for out, when in ((edge_a, odd), (edge_b, jnp.logical_not(odd))):

            @pl.when(when if half == 0 else jnp.logical_not(when))
            def _(out=out):
                for (m, colour), value in found.items():
                    out[m, colour, 0:8] = value[:8]
                    out[m, colour, 8:40] = packed[m, colour, tile]
                    out[m, colour, 40:48] = value[8:]


def load_fine(count, odd, factor, packed, rim, edge_a, edge_b, scaled, ratio, skip, rows):
    used = slice(skip, skip + rows)

    def put(tile, take):
        out = []
        for colour in range(2):
            coef = take(3, colour)
            inside = coef > 0.0
            for m in range(3):
                inverse = jnp.where(inside, 1.0 / (coef + 6.0 * factor[m]), 0.0)
                out.append((m, colour, take(m, colour) * inverse, factor[m] * inverse))
        for m, colour, first, second in out:
            scaled[m, colour, tile] = first
            ratio[m, colour, tile] = second

    def own(m, colour, tile):
        start, end = rim[m, colour, tile, skip:8], rim[m, colour, tile, 8 : 16 - skip]
        return jnp.concatenate([start, packed[m, colour, tile], end], axis=0)

    for tile in range(TILES):
        put(tile + 2, lambda m, colour: own(m, colour, tile))
    none = jnp.zeros((3, 2, rows, 128), F32)
    tile = WIDE - 2
    scaled[:, :, tile] = none
    ratio[:, :, tile] = none
    end = 2 * count + 2
    put(jnp.where(odd, 1, end), lambda m, colour: edge_a[m, colour, used])
    put(jnp.where(odd, end, 1), lambda m, colour: edge_b[m, colour, used])


def clear_rim(values, rows):
    rim = jnp.zeros((3, WIDE, 8, 128), F32)
    values[:, :, 0:8] = rim
    values[:, :, 8 + rows : 16 + rows] = rim
    side = jnp.zeros((3, rows, 128), F32)
    for tile in (0, WIDE - 1):
        values[:, tile, 8 : 8 + rows] = side


def fine_update(other, scaled, ratio, m, colour, tile, chunk, masks):
    lane_low, lane_high, even, edges = masks
    row = 8 + 8 * chunk
    here = other[m, tile, row : row + 8]
    total = here + other[m, tile, row - 1 : row + 7]
    total = total + other[m, tile, row + 1 : row + 9]
    before = other[m, tile - 1, row : row + 8]
    after = other[m, tile + 1, row : row + 8]
    total = total + pltpu.roll(jnp.where(lane_high, before, here), 16, 1)
    total = total + pltpu.roll(jnp.where(lane_low, after, here), 112, 1)
    up, down = pltpu.roll(here, 1, 1), pltpu.roll(here, 127, 1)
    beside = jnp.where(even, up, down) if colour == 0 else jnp.where(even, down, up)
    total = total + jnp.where(edges[colour], 0.0, beside)
    rows = slice(8 * chunk, 8 * chunk + 8)
    return scaled[m, colour, tile, rows] + ratio[m, colour, tile, rows] * total


def fine_masks():
    lane = iota((8, 128), 1)
    even = even_cells(8)
    first, last = lane % 16 == 0, lane % 16 == 15
    edges = (
        (even & first) | (jnp.logical_not(even) & last),
        (even & last) | (jnp.logical_not(even) & first),
    )
    return lane < 16, lane >= 112, even, edges


def fine_sweep(values, scaled, ratio, colour, masks, chunks, tiles=range(1, WIDE - 1)):
    for tile in tiles:
        for m in range(3):
            for chunk in chunks:
                values[colour][m, tile, 8 + 8 * chunk : 16 + 8 * chunk] = fine_update(
                    values[1 - colour], scaled, ratio, m, colour, tile, chunk, masks
                )


def down_kernel(
    info, factor, packed, rim, edge_a, edge_b, pre_red, pre_black, coarse, layers_a, layers_b,
    partial, scaled, ratio, red, black, remain
):
    held, odd, odd_slab = info[0], info[2] == 1, info[3] == 1
    load_fine(held, odd, factor, packed, rim, edge_a, edge_b, scaled, ratio, 0, ROWS)
    masks = fine_masks()
    pre = (red, black)
    clear_rim(red, ROWS)
    clear_rim(black, ROWS)
    chunks = range(ROWS // 8)
    red[:, 1 : WIDE - 1, 8 : 8 + ROWS] = scaled[:, 0, 1 : WIDE - 1]
    fine_sweep(pre, scaled, ratio, 1, masks, chunks)
    fine_sweep(pre, scaled, ratio, 0, masks, chunks)
    fine_sweep(pre, scaled, ratio, 1, masks, chunks)

    skip = (ROWS - NARROW) // 2
    pre_red[...] = red[:, 1 : WIDE - 1, 8 + skip : 8 + skip + NARROW]
    pre_black[...] = black[:, 1 : WIDE - 1, 8 + skip : 8 + skip + NARROW]

    totals = [jnp.zeros((8, 128), F32) for _ in range(4)]
    for tile in range(2, 2 + TILES):
        for chunk in range(1, 5):
            row = 8 + 8 * chunk
            out = slice(8 * chunk - 8, 8 * chunk)
            coef = packed[3, 0, tile - 2, out]
            for m in range(3):
                reds = red[m, tile, row : row + 8]
                blacks = black[m, tile, row : row + 8]
                update = fine_update(black, scaled, ratio, m, 0, tile, chunk, masks)
                left = (coef + 6.0 * factor[m]) * (update - reds)
                left = jnp.where(tile < 2 * held + 2, left, 0.0)
                remain[m, tile - 2, out] = left
                term = (packed[m, 0, tile - 2, out] + left) * reds
                totals[m] = totals[m] + term
                totals[3] = totals[3] + packed[m, 1, tile - 2, out] * blacks
            remain[3, tile - 2, out] = coef + packed[3, 1, tile - 2, out]
    partial[...] = (totals[0] + totals[1]) + (totals[2] + totals[3])
    pool = pool_matrix()
    for slot in range(SLOTS):
        sides = []
        for tile in (2 * slot, 2 * slot + 1):
            sides.append(
                jnp.concatenate(
                    [
                        remain[m, tile, pl.ds(0, COWN, stride=2)]
                        + remain[m, tile, pl.ds(1, COWN, stride=2)]
                        for m in range(4)
                    ],
                    axis=0,
                )
            )
        pooled = exact_dot(jnp.concatenate(sides, axis=1), pool) * 0.125
        for m in range(4):
            box = pooled[COWN * m : COWN * m + COWN]
            coarse[m, slot] = box
            start, end = box[:CHALO], box[COWN - CHALO :]
            rows = slice(CHALO * slot, CHALO * slot + CHALO)
            layers_a[m, rows] = jnp.where(odd_slab, start, end)
            layers_b[m, rows] = jnp.where(odd_slab, end, start)


def edges_kernel(info, coarse, layers_a, layers_b, kept_red, kept_black, edge_a, edge_b):
    held, odd, odd_slab = info[0], info[2] == 1, info[3] == 1

    def fill(out, slots):
        for n, slot in enumerate(slots):
            rows = slice(CHALO * slot, CHALO * slot + CHALO)
            base = CROWS * n
            for m in range(4):
                one, other = layers_a[m, rows], layers_b[m, rows]
                out[m, base : base + CHALO] = jnp.where(odd_slab, one, other)
                out[m, base + CHALO : base + CHALO + COWN] = coarse[m, slot]
                out[m, base + CHALO + COWN : base + CROWS] = jnp.where(odd_slab, other, one)

    for is_odd in (False, True):
        for count in range(2, SLOTS + 1):

            @pl.when((odd == is_odd) & (held == count))
            def _(is_odd=is_odd, count=count):
                start, end = (0, 1), (count - 2, count - 1)
                fill(edge_a, start if is_odd else end)
                fill(edge_b, end if is_odd else start)


def solve_kernel(
    info, factor, previous, coarse, layers_a, layers_b, coarse_a, coarse_b, partial, kept_red,
    kept_black, wanted, share, cscaled, cratio, cred, cblack
):
    held, odd, odd_slab = info[0], info[2] == 1, info[3] == 1

    def put(tile, row, pieces):
        coef = pieces[3]
        size = coef.shape[0]
        for m in range(3):
            b = 0.25 * factor[m]
            inverse = jnp.where(coef > 0.0, 1.0 / (coef + 6.0 * b), 0.0)
            cscaled[m, tile, row : row + size] = pieces[m] * inverse
            cratio[m, tile, row : row + size] = b * inverse

    rest = jnp.zeros((3, CWIDE, 40 - CROWS, 128), F32)
    cscaled[:, :, CROWS:] = rest
    cratio[:, :, CROWS:] = rest
    none = jnp.zeros((3, CROWS, 128), F32)
    for tile in (0, CWIDE - 3, CWIDE - 2, CWIDE - 1):
        cscaled[:, tile, :CROWS] = none
        cratio[:, tile, :CROWS] = none
    for slot in range(SLOTS):
        rows = slice(CHALO * slot, CHALO * slot + CHALO)
        ones = [layers_a[m, rows] for m in range(4)]
        others = [layers_b[m, rows] for m in range(4)]
        above = [jnp.where(odd_slab, ones[m], others[m]) for m in range(4)]
        below = [jnp.where(odd_slab, others[m], ones[m]) for m in range(4)]
        put(slot + 3, 0, above)
        put(slot + 3, CHALO, [coarse[m, slot] for m in range(4)])
        put(slot + 3, CHALO + COWN, below)
    for side in range(2):
        rows = slice(CROWS * side, CROWS * side + CROWS)
        put(jnp.where(odd, 1, held + 3) + side, 0, [coarse_a[m, rows] for m in range(4)])
        put(jnp.where(odd, held + 3, 1) + side, 0, [coarse_b[m, rows] for m in range(4)])

    lane = iota((8, 128), 1)
    lane_low, lane_high = lane < 16, lane >= 112
    first, last = lane % 16 == 0, lane % 16 == 15
    is_red = (iota((8, 128), 0) + lane // 16 + lane % 16) % 2 == 0
    chosen = (is_red, jnp.logical_not(is_red))
    corr = (cred, cblack)
    rim = jnp.zeros((3, CWIDE, 8, 128), F32)
    side = jnp.zeros((3, 40, 128), F32)
    for value in corr:
        value[:, :, 0:8] = rim
        value[:, :, 48:56] = rim
    for tile in (0, CWIDE - 1):
        cred[:, tile, 8:48] = side
    for tile in (0, 1, CWIDE - 2, CWIDE - 1):
        cblack[:, tile, 8:48] = side
    for tile in range(1, CWIDE - 1):
        for m in range(3):
            for chunk in range(5):
                cred[m, tile, 8 + 8 * chunk : 16 + 8 * chunk] = jnp.where(
                    is_red, cscaled[m, tile, 8 * chunk : 8 * chunk + 8], 0.0
                )

    def coarse_sweep(colour, chunks):
        other = corr[1 - colour]
        for tile in range(2, CWIDE - 2):
            for m in range(3):
                for chunk in chunks:
                    row = 8 + 8 * chunk
                    here = other[m, tile, row : row + 8]
                    total = other[m, tile, row - 1 : row + 7] + other[m, tile, row + 1 : row + 9]
                    before = other[m, tile - 1, row : row + 8]
                    after = other[m, tile + 1, row : row + 8]
                    total = total + pltpu.roll(jnp.where(lane_high, before, here), 16, 1)
                    total = total + pltpu.roll(jnp.where(lane_low, after, here), 112, 1)
                    total = total + jnp.where(first, 0.0, pltpu.roll(here, 1, 1))
                    total = total + jnp.where(last, 0.0, pltpu.roll(here, 127, 1))
                    rows = slice(8 * chunk, 8 * chunk + 8)
                    new = cscaled[m, tile, rows] + cratio[m, tile, rows] * total
                    corr[colour][m, tile, row : row + 8] = jnp.where(chosen[colour], new, 0.0)

    for sweep, chunks in enumerate((5, 5, 4, 4, 4, 4)):
        coarse_sweep((sweep + 1) % 2, range(chunks))
    coarse_sweep(1, range(1, 4))

    total = partial[...]
    for slot in range(SLOTS):
        for m in range(3):
            for chunk in range(2):
                row = 8 + CHALO + 8 * chunk
                both = cred[m, slot + 3, row : row + 8] + cblack[m, slot + 3, row : row + 8]
                total = total + 8.0 * (coarse[m, slot, 8 * chunk : 8 * chunk + 8] * both)
    cells = jnp.full((1, 128), info[1], jnp.int32).astype(F32)
    cells = cells * (3.0 * lax.axis_size(SLAB_AXIS) * 32 * 512)
    part = jnp.sum(total, axis=0, keepdims=True) / cells / previous[0]
    share[...] = jnp.broadcast_to(part, share.shape)

    low = 8 + CHALO - 2
    for ctile in range(2, CWIDE - 2):
        for m in range(3):
            wanted[ctile - 2, NARROW // 2 * m : NARROW // 2 * (m + 1)] = (
                cred[m, ctile, low : low + NARROW // 2] + cblack[m, ctile, low : low + NARROW // 2]
            )


def up_kernel(
    info, factor, packed, rim, edge_a, edge_b, pre_red, pre_black, wanted, old, smoothed, carried,
    scaled, ratio, red, black, spread, filled, sem
):
    carry = pltpu.make_async_copy(old, carried, sem.at[SLOTS])
    carry.start()
    held, odd = info[0], info[2] == 1
    skip = (ROWS - NARROW) // 2
    load_fine(held, odd, factor, packed, rim, edge_a, edge_b, scaled, ratio, skip, NARROW)
    masks = fine_masks()
    values = (red, black)
    clear_rim(red, NARROW)
    clear_rim(black, NARROW)
    widen = spread_matrix()
    half_rows = NARROW // 2
    for ctile in range(2, CWIDE - 2):
        wide = exact_dot(wanted[ctile - 2], widen)
        for half in range(2):
            tile = 2 * (ctile - 3) + half + 2
            if not 1 <= tile <= WIDE - 2:
                continue
            for m in range(3):
                piece = wide[half_rows * m : half_rows * m + half_rows, 128 * half : 128 * half + 128]
                spread[m, tile, pl.ds(0, half_rows, stride=2)] = piece
                spread[m, tile, pl.ds(1, half_rows, stride=2)] = piece
    for value, old in ((red, pre_red), (black, pre_black)):
        for tile in range(1, WIDE - 1):
            for m in range(3):
                value[m, tile, 8 : 8 + NARROW] = old[m, tile - 1] + spread[m, tile]
    chunks = range(NARROW // 8)
    for _ in range(2):
        fine_sweep(values, scaled, ratio, 1, masks, chunks)
        fine_sweep(values, scaled, ratio, 0, masks, chunks)

    merge = merge_matrix()
    even = even_cells(3 * 32)
    own = slice(12, 44)
    copies = []
    for slot in range(SLOTS):
        live = slot < held
        for half in range(2):
            tile = 2 + 2 * slot + half
            reds = jnp.concatenate([red[m, tile, own] for m in range(3)], axis=0)
            blacks = jnp.concatenate([black[m, tile, own] for m in range(3)], axis=0)
            both = jnp.concatenate(
                [jnp.where(even, reds, blacks), jnp.where(even, blacks, reds)], axis=1
            )
            cells = exact_dot(jnp.where(live, both, 0.0), merge)
            for m in range(3):
                lanes = slice(256 * half, 256 * half + 256)
                filled[slot, m, :, lanes] = cells[32 * m : 32 * m + 32]
        copies.append(pltpu.make_async_copy(filled.at[slot], smoothed.at[slot], sem.at[slot]))
        copies[-1].start()
    for copy in copies + [carry]:
        copy.wait()


def add_kernel(shares, kept_red, kept_black, kept, total):
    total[...] = jnp.broadcast_to(jnp.sum(shares[...], axis=0, keepdims=True), total.shape)


def direction_kernel(
    info, shares, smoothed, old, same, direction, ready, ready_old, filled, sem
):
    held = info[0]
    fetches = []
    for slot in range(SLOTS):
        fetch = pltpu.make_async_copy(smoothed.at[slot], ready.at[slot], sem.at[slot])
        fetch_old = pltpu.make_async_copy(old.at[slot], ready_old.at[slot], sem.at[SLOTS + slot])
        fetch.start()
        fetch_old.start()
        fetches.append((fetch, fetch_old))
    ratio = jnp.sum(shares[...])
    copies = []
    for slot in range(SLOTS):
        for fetch in fetches[slot]:
            fetch.wait()
        filled[slot] = jnp.where(slot < held, ready[slot] + ratio * ready_old[slot], 0.0)
        target = direction.at[slot]
        copies.append(pltpu.make_async_copy(filled.at[slot], target, sem.at[2 * SLOTS + slot]))
        copies[-1].start()
    for copy in copies:
        copy.wait()


def shape(*dims):
    return jax.ShapeDtypeStruct(dims, F32)


SMEM = pl.BlockSpec(memory_space=pltpu.SMEM)
WHOLE = pl.BlockSpec(memory_space=pltpu.VMEM)
ANYWHERE = pl.BlockSpec(memory_space=pl.ANY)
IN_HBM = pl.BlockSpec(memory_space=pltpu.HBM)


def slot_block(*dims):
    return pl.BlockSpec((1,) + dims, lambda q: (q,) + (0,) * len(dims))


def per_device(box_counts, viscosity, implicit_coef, right_side, old_direction, previous_dot):
    group_n = lax.axis_size(GROUP_AXES)
    slab_n = lax.axis_size(SLAB_AXIS)
    right, coef = right_side[0], implicit_coef[0]
    params = pltpu.CompilerParams(vmem_limit_bytes=VMEM_BYTES)

    place = lax.axis_index(GROUP_AXES)
    info = jnp.stack(
        [
            lax.dynamic_index_in_dim(box_counts, place, 0, keepdims=False),
            jnp.sum(box_counts),
            place % 2,
            lax.axis_index(SLAB_AXIS) % 2,
        ]
    ).astype(jnp.int32)

    top = jnp.concatenate([right[:, :, :8], coef[:, None, :8]], axis=1)
    bottom = jnp.concatenate([right[:, :, 24:], coef[:, None, 24:]], axis=1)
    above = lax.ppermute(bottom, SLAB_AXIS, [(i, i + 1) for i in range(slab_n - 1)])
    below = lax.ppermute(top, SLAB_AXIS, [(i + 1, i) for i in range(slab_n - 1)])

    packed = pl.pallas_call(
        pack_kernel,
        grid=(SLOTS,),
        in_specs=[SMEM, slot_block(3, 32, 512), slot_block(32, 512)],
        out_specs=pl.BlockSpec((4, 2, 2, 32, 128), lambda q: (0, 0, q, 0, 0)),
        out_shape=shape(4, 2, TILES, 32, 128),
        compiler_params=params,
        cost_estimate=pl.CostEstimate(flops=20000000, bytes_accessed=2000000, transcendentals=0),
        name="pack",
    )(info, right, coef)
    edges = pl.pallas_call(
        pack_edges_kernel,
        in_specs=[SMEM] + [WHOLE] * 3,
        out_specs=[WHOLE] * 2,
        out_shape=[shape(4, 2, ROWS, 128)] * 2,
        compiler_params=params,
        name="pack_edges",
    )(info, above, below, packed)
    edges = exchange(*edges, GROUP_AXES)
    rim = pl.pallas_call(
        pack_rim_kernel,
        in_specs=[SMEM] + [WHOLE] * 2,
        out_specs=WHOLE,
        out_shape=shape(4, 2, TILES, 16, 128),
        compiler_params=params,
        cost_estimate=pl.CostEstimate(flops=10000000, bytes_accessed=1000000, transcendentals=0),
        name="pack_rim",
    )(info, above, below)

    padded = pltpu.VMEM((3, WIDE, ROWS + 16, 128), F32)
    pre_shape = shape(3, WIDE - 2, NARROW, 128)
    fine = pltpu.VMEM((3, 2, WIDE, ROWS, 128), F32)
    layer_shape = shape(4, SLOTS * CHALO, 128)
    pre_red, pre_black, coarse, *layers, partial = pl.pallas_call(
        down_kernel,
        in_specs=[SMEM] * 2 + [WHOLE] * 4,
        out_specs=[WHOLE] * 6,
        out_shape=[
            pre_shape,
            pre_shape,
            shape(4, SLOTS, COWN, 128),
            layer_shape,
            layer_shape,
            shape(8, 128),
        ],
        scratch_shapes=[fine, fine, padded, padded, pltpu.VMEM((4, TILES, 32, 128), F32)],
        compiler_params=params,
        name="down",
    )(info, viscosity, packed, rim, *edges)

    layers = exchange(*layers, SLAB_AXIS)
    coarse_edges = pl.pallas_call(
        edges_kernel,
        in_specs=[SMEM] + [WHOLE] * 5,
        out_specs=[WHOLE] * 2,
        out_shape=[shape(4, 2 * CROWS, 128)] * 2,
        compiler_params=params,
        name="edges",
    )(info, coarse, *layers, pre_red, pre_black)
    coarse_edges = exchange(*coarse_edges, GROUP_AXES)

    narrow = pltpu.VMEM((3, 2, WIDE, NARROW, 128), F32)
    value = pltpu.VMEM((3, WIDE, NARROW + 16, 128), F32)
    cfine = pltpu.VMEM((3, CWIDE, 40, 128), F32)
    cvalue = pltpu.VMEM((3, CWIDE, 56, 128), F32)
    wanted, share = pl.pallas_call(
        solve_kernel,
        in_specs=[SMEM] * 3 + [WHOLE] * 8,
        out_specs=[WHOLE] * 2,
        out_shape=[shape(CWIDE - 4, 3 * NARROW // 2, 128), shape(group_n, 128)],
        scratch_shapes=[cfine, cfine, cvalue, cvalue],
        compiler_params=params,
        name="solve",
    )(info, viscosity, previous_dot, coarse, *layers, *coarse_edges, partial, pre_red, pre_black)

    whole = shape(SLOTS, 3, 32, 512)
    held_whole = pltpu.VMEM((SLOTS, 3, 32, 512), F32)
    smoothed, carried = pl.pallas_call(
        up_kernel,
        in_specs=[SMEM] * 2 + [WHOLE] * 7 + [ANYWHERE],
        out_specs=[IN_HBM] * 2,
        out_shape=[whole] * 2,
        scratch_shapes=[
            narrow,
            narrow,
            value,
            value,
            pltpu.VMEM((3, WIDE, NARROW, 128), F32),
            held_whole,
            pltpu.SemaphoreType.DMA((SLOTS + 1,)),
        ],
        compiler_params=params,
        cost_estimate=pl.CostEstimate(flops=40000000, bytes_accessed=8000000, transcendentals=0),
        name="up",
    )(
        info, viscosity, packed, rim, *edges, pre_red, pre_black, wanted, old_direction[0]
    )

    shares = lax.all_to_all(share, GROUP_AXES, 0, 0)
    shares = pl.pallas_call(
        add_kernel,
        in_specs=[WHOLE] * 4,
        out_specs=WHOLE,
        out_shape=shape(slab_n, 128),
        compiler_params=params,
        name="add",
    )(shares, pre_red, pre_black, wanted)
    shares = lax.all_to_all(shares, SLAB_AXIS, 0, 0)
    smoothed, direction = pl.pallas_call(
        direction_kernel,
        in_specs=[SMEM, WHOLE, IN_HBM, IN_HBM],
        out_specs=[IN_HBM] * 2,
        out_shape=[whole] * 2,
        input_output_aliases={2: 0, 3: 1},
        scratch_shapes=[held_whole] * 3 + [pltpu.SemaphoreType.DMA((3 * SLOTS,))],
        compiler_params=params,
        name="direction",
    )(info, shares, smoothed, carried)
    return smoothed[None], direction[None]


def solution(mesh):
    wide = P("gx", GROUP_AXES, None, None, None)
    placed = (P(), P(), P("gx", GROUP_AXES, None, None), wide, wide, P())
    return jax.shard_map(
        per_device, mesh=mesh, in_specs=placed, out_specs=(wide, wide), check_vma=False
    )
```

```python
import functools

import jax
import jax.numpy as jnp
from jax import lax
from jax.experimental import pallas as pl
from jax.experimental.pallas import tpu as pltpu
from jax.sharding import PartitionSpec as P

GROUP_AXES = ("gy", "gz")
SLAB_AXIS = "gx"
F32 = jnp.float32
BF16 = jnp.bfloat16
VMEM_BYTES = 12 * 1024 * 1024

SLOTS = 4
TILES = 2 * SLOTS
ROWS = 48
NARROW = 40
WIDE = TILES + 4
COWN = 16
CHALO = 10
CROWS = COWN + 2 * CHALO
EXTRA_ROWS = (0, 8, 16, 24, 28)
CWIDE = SLOTS + 6


def iota(shape, dim):
    return lax.broadcasted_iota(jnp.int32, shape, dim)


def exact_dot(values, ones):
    high = values.astype(BF16)
    rest = values - high.astype(F32)
    mid = rest.astype(BF16)
    low = (rest - mid.astype(F32)).astype(BF16)
    total = jnp.dot(low, ones, preferred_element_type=F32)
    total = total + jnp.dot(mid, ones, preferred_element_type=F32)
    return total + jnp.dot(high, ones, preferred_element_type=F32)


def split_matrix():
    source, target = iota((256, 256), 0), iota((256, 256), 1)
    y = source % 32
    wanted = (y % 2) * 128 + source // 32 * 16 + y // 2
    return (target == wanted).astype(F32).astype(BF16)


def merge_matrix():
    source, target = iota((256, 256), 0), iota((256, 256), 1)
    y = target % 32
    wanted = (y % 2) * 128 + target // 32 * 16 + y // 2
    return (source == wanted).astype(F32).astype(BF16)


def pool_matrix():
    source, target = iota((256, 128), 0), iota((256, 128), 1)
    wanted = source // 32 * 16 + source % 16
    return (target == wanted).astype(F32).astype(BF16)


def spread_matrix():
    source, target = iota((128, 256), 0), iota((128, 256), 1)
    wanted = target // 32 * 16 + target % 16
    return (source == wanted).astype(F32).astype(BF16)


def even_cells(rows):
    shape = (rows, 128)
    return (iota(shape, 0) + iota(shape, 1) // 16) % 2 == 0


def swap(value, axis, offset):
    size = lax.axis_size(axis)
    pairs = []
    for i in range(offset, size - 1, 2):
        pairs += [(i, i + 1), (i + 1, i)]
    return lax.ppermute(value, axis, pairs)


def exchange(first, second, axis):
    return swap(first, axis, 0), swap(second, axis, 1)


def split_cells(cells, rows, packed, put):
    even = even_cells(4 * rows)
    both = exact_dot(cells, packed)
    first, second = both[:, :128], both[:, 128:]
    red = jnp.where(even, first, second)
    black = jnp.where(even, second, first)
    for m in range(4):
        put(m, 0, red[rows * m : rows * m + rows])
        put(m, 1, black[rows * m : rows * m + rows])


def pack_kernel(info, right, coef, packed):
    live = pl.program_id(0) < info[0]
    split = split_matrix()
    for half in range(2):
        lanes = slice(256 * half, 256 * half + 256)
        parts = [right[0, m, :, lanes] for m in range(3)] + [coef[0, :, lanes]]
        cells = jnp.where(live, jnp.concatenate(parts, axis=0), 0.0)

        def put(m, colour, value, half=half):
            packed[m, colour, half] = value

        split_cells(cells, 32, split, put)


def pack_rim_kernel(info, above, below, rim):
    held = info[0]
    split = split_matrix()
    for slot in range(SLOTS):
        for half in range(2):
            lanes = slice(256 * half, 256 * half + 256)
            parts = []
            for m in range(4):
                parts += [above[slot, m, :, lanes], below[slot, m, :, lanes]]
            cells = jnp.where(slot < held, jnp.concatenate(parts, axis=0), 0.0)

            def put(m, colour, value, tile=2 * slot + half):
                rim[m, colour, tile] = value

            split_cells(cells, 16, split, put)


def pack_edges_kernel(info, above, below, packed, edge_a, edge_b):
    held, odd = info[0], info[2] == 1
    parts, found = [], {}
    places = ((0, 0), (held - 1, 1))
    for m in range(4):
        for slot, half in places:
            lanes = slice(256 * half, 256 * half + 256)
            parts += [above[slot, m, :, lanes], below[slot, m, :, lanes]]

    def put(m, colour, value):
        found[m, colour] = value

    split_cells(jnp.concatenate(parts, axis=0), 32, split_matrix(), put)
    for slot, half in places:
        tile = 2 * slot + half
        for out, when in ((edge_a, odd), (edge_b, jnp.logical_not(odd))):

            @pl.when(when if half == 0 else jnp.logical_not(when))
            def _(out=out):
                for (m, colour), value in found.items():
                    out[m, colour, 0:8] = value[16 * half : 16 * half + 8]
                    out[m, colour, 8:40] = packed[m, colour, tile]
                    out[m, colour, 40:48] = value[16 * half + 8 : 16 * half + 16]


def load_fine(count, odd, factor, packed, rim, edge_a, edge_b, scaled, ratio, skip, rows):
    used = slice(skip, skip + rows)

    def put(tile, take):
        out = []
        for colour in range(2):
            coef = take(3, colour)
            inside = coef > 0.0
            for m in range(3):
                inverse = jnp.where(inside, 1.0 / (coef + 6.0 * factor[m]), 0.0)
                out.append((m, colour, take(m, colour) * inverse, factor[m] * inverse))
        for m, colour, first, second in out:
            scaled[m, colour, tile] = first
            ratio[m, colour, tile] = second

    def own(m, colour, tile):
        start, end = rim[m, colour, tile, skip:8], rim[m, colour, tile, 8 : 16 - skip]
        return jnp.concatenate([start, packed[m, colour, tile], end], axis=0)

    for tile in range(TILES):
        put(tile + 2, lambda m, colour: own(m, colour, tile))
    none = jnp.zeros((3, 2, rows, 128), F32)
    tile = WIDE - 2
    scaled[:, :, tile] = none
    ratio[:, :, tile] = none
    end = 2 * count + 2
    put(jnp.where(odd, 1, end), lambda m, colour: edge_a[m, colour, used])
    put(jnp.where(odd, end, 1), lambda m, colour: edge_b[m, colour, used])


def clear_rim(values, rows):
    rim = jnp.zeros((3, WIDE, 8, 128), F32)
    values[:, :, 0:8] = rim
    values[:, :, 8 + rows : 16 + rows] = rim
    side = jnp.zeros((3, rows, 128), F32)
    for tile in (0, WIDE - 1):
        values[:, tile, 8 : 8 + rows] = side


def fine_update(other, scaled, ratio, m, colour, tile, chunk, masks):
    lane_low, lane_high, even, edges = masks
    row = 8 + 8 * chunk
    here = other[m, tile, row : row + 8]
    total = here + other[m, tile, row - 1 : row + 7]
    total = total + other[m, tile, row + 1 : row + 9]
    before = other[m, tile - 1, row : row + 8]
    after = other[m, tile + 1, row : row + 8]
    total = total + pltpu.roll(jnp.where(lane_high, before, here), 16, 1)
    total = total + pltpu.roll(jnp.where(lane_low, after, here), 112, 1)
    up, down = pltpu.roll(here, 1, 1), pltpu.roll(here, 127, 1)
    beside = jnp.where(even, up, down) if colour == 0 else jnp.where(even, down, up)
    total = total + jnp.where(edges[colour], 0.0, beside)
    rows = slice(8 * chunk, 8 * chunk + 8)
    return scaled[m, colour, tile, rows] + ratio[m, colour, tile, rows] * total


def fine_masks():
    lane = iota((8, 128), 1)
    even = even_cells(8)
    first, last = lane % 16 == 0, lane % 16 == 15
    edges = (
        (even & first) | (jnp.logical_not(even) & last),
        (even & last) | (jnp.logical_not(even) & first),
    )
    return lane < 16, lane >= 112, even, edges


def fine_sweep(values, scaled, ratio, colour, masks, chunks, tiles=range(1, WIDE - 1)):
    for tile in tiles:
        for m in range(3):
            for chunk in chunks:
                values[colour][m, tile, 8 + 8 * chunk : 16 + 8 * chunk] = fine_update(
                    values[1 - colour], scaled, ratio, m, colour, tile, chunk, masks
                )


def down_kernel(
    info, factor, packed, rim, edge_a, edge_b, red, black, coarse, layers_a, layers_b, remain,
    scaled, ratio
):
    held, odd, odd_slab = info[0], info[2] == 1, info[3] == 1
    load_fine(held, odd, factor, packed, rim, edge_a, edge_b, scaled, ratio, 0, ROWS)
    masks = fine_masks()
    pre = (red, black)
    clear_rim(red, ROWS)
    clear_rim(black, ROWS)
    chunks = range(ROWS // 8)
    red[:, 1 : WIDE - 1, 8 : 8 + ROWS] = scaled[:, 0, 1 : WIDE - 1]
    fine_sweep(pre, scaled, ratio, 1, masks, chunks)
    fine_sweep(pre, scaled, ratio, 0, masks, chunks)
    fine_sweep(pre, scaled, ratio, 1, masks, chunks)

    for tile in range(2, 2 + TILES):
        for chunk in range(1, 5):
            row = 8 + 8 * chunk
            out = slice(8 * chunk - 8, 8 * chunk)
            coef = packed[3, 0, tile - 2, out]
            for m in range(3):
                reds = red[m, tile, row : row + 8]
                update = fine_update(black, scaled, ratio, m, 0, tile, chunk, masks)
                left = (coef + 6.0 * factor[m]) * (update - reds)
                remain[m, tile - 2, out] = jnp.where(tile < 2 * held + 2, left, 0.0)
            remain[3, tile - 2, out] = coef + packed[3, 1, tile - 2, out]
    sides = []
    for half in range(2):
        parts = []
        for tile in range(half, TILES, 2):
            for m in range(4):
                first = remain[m, tile, pl.ds(0, COWN, stride=2)]
                parts.append(first + remain[m, tile, pl.ds(1, COWN, stride=2)])
        sides.append(jnp.concatenate(parts, axis=0))
    pooled = exact_dot(jnp.concatenate(sides, axis=1), pool_matrix()) * 0.125
    for slot in range(SLOTS):
        for m in range(4):
            place = COWN * (4 * slot + m)
            box = pooled[place : place + COWN]
            coarse[m, slot] = box
            start, end = box[:CHALO], box[COWN - CHALO :]
            rows = slice(CHALO * slot, CHALO * slot + CHALO)
            layers_a[m, rows] = jnp.where(odd_slab, start, end)
            layers_b[m, rows] = jnp.where(odd_slab, end, start)


def keep_kernel(packed, red, black, remain, pre_red, pre_black, partial):
    skip = (ROWS - NARROW) // 2
    pre_red[...] = red[:, 1 : WIDE - 1, 8 + skip : 8 + skip + NARROW]
    pre_black[...] = black[:, 1 : WIDE - 1, 8 + skip : 8 + skip + NARROW]
    totals = [jnp.zeros((8, 128), F32) for _ in range(6)]
    for tile in range(TILES):
        for chunk in range(4):
            rows, inner = slice(8 * chunk, 8 * chunk + 8), slice(16 + 8 * chunk, 24 + 8 * chunk)
            for m in range(3):
                both = packed[m, 0, tile, rows] + remain[m, tile, rows]
                totals[m] = totals[m] + both * red[m, tile + 2, inner]
                totals[m + 3] = totals[m + 3] + packed[m, 1, tile, rows] * black[m, tile + 2, inner]
    partial[...] = sum(totals[1:], totals[0])


def edges_kernel(info, coarse, layers_a, layers_b, kept_red, kept_black, edge_a, edge_b, tall):
    held, odd, odd_slab = info[0], info[2] == 1, info[3] == 1

    group = iota((8, 128), 1) // 16

    def fill(out, slot, beside, first):
        for m in range(4):
            for n, source in enumerate((slot, beside)):
                rows = slice(CHALO * source, CHALO * source + CHALO)
                one, other = layers_a[m, rows], layers_b[m, rows]
                target = out if n == 0 else tall
                target[m, 0:CHALO] = jnp.where(odd_slab, one, other)
                target[m, CHALO : CHALO + COWN] = coarse[m, source]
                target[m, CHALO + COWN : CROWS] = jnp.where(odd_slab, other, one)
            extra = jnp.zeros((8, 128), F32)
            out[m, CROWS:40] = extra[: 40 - CROWS]
            for j, row in enumerate(EXTRA_ROWS):
                turn = 16 * j if first else 16 * (j + 1)
                piece = pltpu.roll(tall[m, row : row + 8], turn, 1)
                extra = jnp.where(group == j, piece, extra)
            out[m, 40:48] = extra

    for is_odd in (False, True):
        for count in range(2, SLOTS + 1):

            @pl.when((odd == is_odd) & (held == count))
            def _(is_odd=is_odd, count=count):
                start, end = (0, 1, True), (count - 1, count - 2, False)
                fill(edge_a, *(start if is_odd else end))
                fill(edge_b, *(end if is_odd else start))


def solve_kernel(
    info, factor, previous, coarse, layers_a, layers_b, coarse_a, coarse_b, partial, kept_red,
    kept_black, wanted, share, cscaled, cratio, cred, cblack
):
    held, odd, odd_slab = info[0], info[2] == 1, info[3] == 1

    def put(tile, row, pieces):
        coef = pieces[3]
        size = coef.shape[0]
        for m in range(3):
            b = 0.25 * factor[m]
            inverse = jnp.where(coef > 0.0, 1.0 / (coef + 6.0 * b), 0.0)
            cscaled[m, tile, row : row + size] = pieces[m] * inverse
            cratio[m, tile, row : row + size] = b * inverse

    rest = jnp.zeros((3, CWIDE, 40 - CROWS, 128), F32)
    cscaled[:, :, CROWS:] = rest
    cratio[:, :, CROWS:] = rest
    none = jnp.zeros((3, CROWS, 128), F32)
    for tile in (0, CWIDE - 3, CWIDE - 2, CWIDE - 1):
        cscaled[:, tile, :CROWS] = none
        cratio[:, tile, :CROWS] = none
    for slot in range(SLOTS):
        rows = slice(CHALO * slot, CHALO * slot + CHALO)
        ones = [layers_a[m, rows] for m in range(4)]
        others = [layers_b[m, rows] for m in range(4)]
        above = [jnp.where(odd_slab, ones[m], others[m]) for m in range(4)]
        below = [jnp.where(odd_slab, others[m], ones[m]) for m in range(4)]
        put(slot + 3, 0, above)
        put(slot + 3, CHALO, [coarse[m, slot] for m in range(4)])
        put(slot + 3, CHALO + COWN, below)
    lane = iota((8, 128), 1)
    for edge, is_left in ((coarse_a, odd), (coarse_b, jnp.logical_not(odd))):
        put(jnp.where(is_left, 2, held + 3), 0, [edge[m, 0:CROWS] for m in range(4)])
        tile = jnp.where(is_left, 1, held + 4)
        for j, row in enumerate(EXTRA_ROWS):
            pieces = []
            for m in range(4):
                extra = edge[m, 40:48]
                left = jnp.where(lane >= 112, pltpu.roll(extra, (112 - 16 * j) % 128, 1), 0.0)
                right = jnp.where(lane < 16, pltpu.roll(extra, (128 - 16 * j) % 128, 1), 0.0)
                pieces.append(jnp.where(is_left, left, right))
            put(tile, row, pieces)

    lane_low, lane_high = lane < 16, lane >= 112
    first, last = lane % 16 == 0, lane % 16 == 15
    is_red = (iota((8, 128), 0) + lane // 16 + lane % 16) % 2 == 0
    chosen = (is_red, jnp.logical_not(is_red))
    corr = (cred, cblack)
    rim = jnp.zeros((3, CWIDE, 8, 128), F32)
    side = jnp.zeros((3, 40, 128), F32)
    for value in corr:
        value[:, :, 0:8] = rim
        value[:, :, 48:56] = rim
    for tile in (0, CWIDE - 1):
        cred[:, tile, 8:48] = side
    for tile in (0, 1, CWIDE - 2, CWIDE - 1):
        cblack[:, tile, 8:48] = side
    for tile in range(1, CWIDE - 1):
        for m in range(3):
            for chunk in range(5):
                cred[m, tile, 8 + 8 * chunk : 16 + 8 * chunk] = jnp.where(
                    is_red, cscaled[m, tile, 8 * chunk : 8 * chunk + 8], 0.0
                )

    def coarse_sweep(colour, chunks):
        other = corr[1 - colour]
        for tile in range(2, CWIDE - 2):
            for m in range(3):
                for chunk in chunks:
                    row = 8 + 8 * chunk
                    here = other[m, tile, row : row + 8]
                    total = other[m, tile, row - 1 : row + 7] + other[m, tile, row + 1 : row + 9]
                    before = other[m, tile - 1, row : row + 8]
                    after = other[m, tile + 1, row : row + 8]
                    total = total + pltpu.roll(jnp.where(lane_high, before, here), 16, 1)
                    total = total + pltpu.roll(jnp.where(lane_low, after, here), 112, 1)
                    total = total + jnp.where(first, 0.0, pltpu.roll(here, 1, 1))
                    total = total + jnp.where(last, 0.0, pltpu.roll(here, 127, 1))
                    rows = slice(8 * chunk, 8 * chunk + 8)
                    new = cscaled[m, tile, rows] + cratio[m, tile, rows] * total
                    corr[colour][m, tile, row : row + 8] = jnp.where(chosen[colour], new, 0.0)

    for sweep, chunks in enumerate((5, 5, 4, 4, 4, 4)):
        coarse_sweep((sweep + 1) % 2, range(chunks))
    coarse_sweep(1, range(1, 4))

    total = partial[...]
    for slot in range(SLOTS):
        for m in range(3):
            for chunk in range(2):
                row = 8 + CHALO + 8 * chunk
                both = cred[m, slot + 3, row : row + 8] + cblack[m, slot + 3, row : row + 8]
                total = total + 8.0 * (coarse[m, slot, 8 * chunk : 8 * chunk + 8] * both)
    cells = jnp.full((1, 128), info[1], jnp.int32).astype(F32)
    cells = cells * (3.0 * lax.axis_size(SLAB_AXIS) * 32 * 512)
    part = jnp.sum(total, axis=0, keepdims=True) / cells / previous[0]
    share[...] = jnp.broadcast_to(part, share.shape)

    low = 8 + CHALO - 2
    for ctile in range(2, CWIDE - 2):
        for m in range(3):
            wanted[ctile - 2, NARROW // 2 * m : NARROW // 2 * (m + 1)] = (
                cred[m, ctile, low : low + NARROW // 2] + cblack[m, ctile, low : low + NARROW // 2]
            )


def up_kernel(
    info, factor, packed, rim, edge_a, edge_b, pre_red, pre_black, wanted, old, smoothed, carried,
    scaled, ratio, red, black, spread, filled, sem
):
    carry = pltpu.make_async_copy(old, carried, sem.at[SLOTS])
    carry.start()
    held, odd = info[0], info[2] == 1
    skip = (ROWS - NARROW) // 2
    load_fine(held, odd, factor, packed, rim, edge_a, edge_b, scaled, ratio, skip, NARROW)
    masks = fine_masks()
    values = (red, black)
    clear_rim(red, NARROW)
    clear_rim(black, NARROW)
    widen = spread_matrix()
    half_rows = NARROW // 2
    for ctile in range(2, CWIDE - 2):
        wide = exact_dot(wanted[ctile - 2], widen)
        for half in range(2):
            tile = 2 * (ctile - 3) + half + 2
            if not 1 <= tile <= WIDE - 2:
                continue
            for m in range(3):
                piece = wide[half_rows * m : half_rows * m + half_rows, 128 * half : 128 * half + 128]
                spread[m, tile, pl.ds(0, half_rows, stride=2)] = piece
                spread[m, tile, pl.ds(1, half_rows, stride=2)] = piece
    for value, old in ((red, pre_red), (black, pre_black)):
        for tile in range(1, WIDE - 1):
            for m in range(3):
                value[m, tile, 8 : 8 + NARROW] = old[m, tile - 1] + spread[m, tile]
    chunks = range(NARROW // 8)
    for _ in range(2):
        fine_sweep(values, scaled, ratio, 1, masks, chunks)
        fine_sweep(values, scaled, ratio, 0, masks, chunks)

    merge = merge_matrix()
    even = even_cells(3 * 32)
    own = slice(12, 44)
    copies = []
    for slot in range(SLOTS):
        live = slot < held
        for half in range(2):
            tile = 2 + 2 * slot + half
            reds = jnp.concatenate([red[m, tile, own] for m in range(3)], axis=0)
            blacks = jnp.concatenate([black[m, tile, own] for m in range(3)], axis=0)
            both = jnp.concatenate(
                [jnp.where(even, reds, blacks), jnp.where(even, blacks, reds)], axis=1
            )
            cells = exact_dot(jnp.where(live, both, 0.0), merge)
            for m in range(3):
                lanes = slice(256 * half, 256 * half + 256)
                filled[slot, m, :, lanes] = cells[32 * m : 32 * m + 32]
        copies.append(pltpu.make_async_copy(filled.at[slot], smoothed.at[slot], sem.at[slot]))
        copies[-1].start()
    for copy in copies + [carry]:
        copy.wait()


def add_kernel(shares, kept_red, kept_black, kept, total):
    total[...] = jnp.broadcast_to(jnp.sum(shares[...], axis=0, keepdims=True), total.shape)


def direction_kernel(
    info, shares, smoothed, old, same, direction, ready, ready_old, filled, sem
):
    held = info[0]
    fetches = []
    for slot in range(SLOTS):
        fetch = pltpu.make_async_copy(smoothed.at[slot], ready.at[slot], sem.at[slot])
        fetch_old = pltpu.make_async_copy(old.at[slot], ready_old.at[slot], sem.at[SLOTS + slot])
        fetch.start()
        fetch_old.start()
        fetches.append((fetch, fetch_old))
    ratio = jnp.sum(shares[...])
    copies = []
    for slot in range(SLOTS):
        for fetch in fetches[slot]:
            fetch.wait()
        filled[slot] = jnp.where(slot < held, ready[slot] + ratio * ready_old[slot], 0.0)
        target = direction.at[slot]
        copies.append(pltpu.make_async_copy(filled.at[slot], target, sem.at[2 * SLOTS + slot]))
        copies[-1].start()
    for copy in copies:
        copy.wait()


def shape(*dims):
    return jax.ShapeDtypeStruct(dims, F32)


SMEM = pl.BlockSpec(memory_space=pltpu.SMEM)
WHOLE = pl.BlockSpec(memory_space=pltpu.VMEM)
ANYWHERE = pl.BlockSpec(memory_space=pl.ANY)
IN_HBM = pl.BlockSpec(memory_space=pltpu.HBM)


def slot_block(*dims):
    return pl.BlockSpec((1,) + dims, lambda q: (q,) + (0,) * len(dims))


def per_device(box_counts, viscosity, implicit_coef, right_side, old_direction, previous_dot):
    group_n = lax.axis_size(GROUP_AXES)
    slab_n = lax.axis_size(SLAB_AXIS)
    right, coef = right_side[0], implicit_coef[0]
    params = pltpu.CompilerParams(vmem_limit_bytes=VMEM_BYTES)

    place = lax.axis_index(GROUP_AXES)
    info = jnp.stack(
        [
            lax.dynamic_index_in_dim(box_counts, place, 0, keepdims=False),
            jnp.sum(box_counts),
            place % 2,
            lax.axis_index(SLAB_AXIS) % 2,
        ]
    ).astype(jnp.int32)

    top = jnp.concatenate([right[:, :, :8], coef[:, None, :8]], axis=1)
    bottom = jnp.concatenate([right[:, :, 24:], coef[:, None, 24:]], axis=1)
    above = lax.ppermute(bottom, SLAB_AXIS, [(i, i + 1) for i in range(slab_n - 1)])
    below = lax.ppermute(top, SLAB_AXIS, [(i + 1, i) for i in range(slab_n - 1)])

    packed = pl.pallas_call(
        pack_kernel,
        grid=(SLOTS,),
        in_specs=[SMEM, slot_block(3, 32, 512), slot_block(32, 512)],
        out_specs=pl.BlockSpec((4, 2, 2, 32, 128), lambda q: (0, 0, q, 0, 0)),
        out_shape=shape(4, 2, TILES, 32, 128),
        compiler_params=params,
        cost_estimate=pl.CostEstimate(flops=20000000, bytes_accessed=2000000, transcendentals=0),
        name="pack",
    )(info, right, coef)
    edges = pl.pallas_call(
        pack_edges_kernel,
        in_specs=[SMEM] + [WHOLE] * 3,
        out_specs=[WHOLE] * 2,
        out_shape=[shape(4, 2, ROWS, 128)] * 2,
        compiler_params=params,
        name="pack_edges",
    )(info, above, below, packed)
    edges = exchange(*edges, GROUP_AXES)
    rim = pl.pallas_call(
        pack_rim_kernel,
        in_specs=[SMEM] + [WHOLE] * 2,
        out_specs=WHOLE,
        out_shape=shape(4, 2, TILES, 16, 128),
        compiler_params=params,
        cost_estimate=pl.CostEstimate(flops=10000000, bytes_accessed=1000000, transcendentals=0),
        name="pack_rim",
    )(info, above, below)

    padded = shape(3, WIDE, ROWS + 16, 128)
    fine = pltpu.VMEM((3, 2, WIDE, ROWS, 128), F32)
    layer_shape = shape(4, SLOTS * CHALO, 128)
    red, black, coarse, *layers, remain = pl.pallas_call(
        down_kernel,
        in_specs=[SMEM] * 2 + [WHOLE] * 4,
        out_specs=[WHOLE] * 6,
        out_shape=[
            padded,
            padded,
            shape(4, SLOTS, COWN, 128),
            layer_shape,
            layer_shape,
            shape(4, TILES, 32, 128),
        ],
        scratch_shapes=[fine, fine],
        compiler_params=params,
        name="down",
    )(info, viscosity, packed, rim, *edges)

    layers = exchange(*layers, SLAB_AXIS)
    pre_red, pre_black, partial = pl.pallas_call(
        keep_kernel,
        in_specs=[WHOLE] * 4,
        out_specs=[WHOLE] * 3,
        out_shape=[shape(3, WIDE - 2, NARROW, 128)] * 2 + [shape(8, 128)],
        compiler_params=params,
        cost_estimate=pl.CostEstimate(flops=4000000, bytes_accessed=1000000, transcendentals=0),
        name="keep",
    )(packed, red, black, remain)
    coarse_edges = pl.pallas_call(
        edges_kernel,
        in_specs=[SMEM] + [WHOLE] * 5,
        out_specs=[WHOLE] * 2,
        out_shape=[shape(4, 48, 128)] * 2,
        scratch_shapes=[pltpu.VMEM((4, 40, 128), F32)],
        compiler_params=params,
        name="edges",
    )(info, coarse, *layers, pre_red, pre_black)
    coarse_edges = exchange(*coarse_edges, GROUP_AXES)

    narrow = pltpu.VMEM((3, 2, WIDE, NARROW, 128), F32)
    value = pltpu.VMEM((3, WIDE, NARROW + 16, 128), F32)
    cfine = pltpu.VMEM((3, CWIDE, 40, 128), F32)
    cvalue = pltpu.VMEM((3, CWIDE, 56, 128), F32)
    wanted, share = pl.pallas_call(
        solve_kernel,
        in_specs=[SMEM] * 3 + [WHOLE] * 8,
        out_specs=[WHOLE] * 2,
        out_shape=[shape(CWIDE - 4, 3 * NARROW // 2, 128), shape(group_n, 128)],
        scratch_shapes=[cfine, cfine, cvalue, cvalue],
        compiler_params=params,
        name="solve",
    )(info, viscosity, previous_dot, coarse, *layers, *coarse_edges, partial, pre_red, pre_black)

    whole = shape(SLOTS, 3, 32, 512)
    held_whole = pltpu.VMEM((SLOTS, 3, 32, 512), F32)
    smoothed, carried = pl.pallas_call(
        up_kernel,
        in_specs=[SMEM] * 2 + [WHOLE] * 7 + [ANYWHERE],
        out_specs=[IN_HBM] * 2,
        out_shape=[whole] * 2,
        scratch_shapes=[
            narrow,
            narrow,
            value,
            value,
            pltpu.VMEM((3, WIDE, NARROW, 128), F32),
            held_whole,
            pltpu.SemaphoreType.DMA((SLOTS + 1,)),
        ],
        compiler_params=params,
        cost_estimate=pl.CostEstimate(flops=40000000, bytes_accessed=8000000, transcendentals=0),
        name="up",
    )(
        info, viscosity, packed, rim, *edges, pre_red, pre_black, wanted, old_direction[0]
    )

    shares = lax.all_to_all(share, GROUP_AXES, 0, 0)
    shares = pl.pallas_call(
        add_kernel,
        in_specs=[WHOLE] * 4,
        out_specs=WHOLE,
        out_shape=shape(slab_n, 128),
        compiler_params=params,
        name="add",
    )(shares, pre_red, pre_black, wanted)
    shares = lax.all_to_all(shares, SLAB_AXIS, 0, 0)
    smoothed, direction = pl.pallas_call(
        direction_kernel,
        in_specs=[SMEM, WHOLE, IN_HBM, IN_HBM],
        out_specs=[IN_HBM] * 2,
        out_shape=[whole] * 2,
        input_output_aliases={2: 0, 3: 1},
        scratch_shapes=[held_whole] * 3 + [pltpu.SemaphoreType.DMA((3 * SLOTS,))],
        compiler_params=params,
        name="direction",
    )(info, shares, smoothed, carried)
    return smoothed[None], direction[None]


def solution(mesh):
    wide = P("gx", GROUP_AXES, None, None, None)
    placed = (P(), P(), P("gx", GROUP_AXES, None, None), wide, wide, P())
    return jax.shard_map(
        per_device, mesh=mesh, in_specs=placed, out_specs=(wide, wide), check_vma=False
    )
```

```python
import functools

import jax
import jax.numpy as jnp
from jax import lax
from jax.experimental import pallas as pl
from jax.experimental.pallas import tpu as pltpu
from jax.sharding import PartitionSpec as P

GROUP_AXES = ("gy", "gz")
SLAB_AXIS = "gx"
F32 = jnp.float32
BF16 = jnp.bfloat16
VMEM_BYTES = 12 * 1024 * 1024

SLOTS = 4
TILES = 2 * SLOTS
ROWS = 48
NARROW = 40
WIDE = TILES + 4
COWN = 16
CHALO = 10
CROWS = COWN + 2 * CHALO
EXTRA_ROWS = (0, 8, 16, 24, 28)
CWIDE = SLOTS + 6


def iota(shape, dim):
    return lax.broadcasted_iota(jnp.int32, shape, dim)


def exact_dot(values, ones):
    high = values.astype(BF16)
    rest = values - high.astype(F32)
    mid = rest.astype(BF16)
    low = (rest - mid.astype(F32)).astype(BF16)
    total = jnp.dot(low, ones, preferred_element_type=F32)
    total = total + jnp.dot(mid, ones, preferred_element_type=F32)
    return total + jnp.dot(high, ones, preferred_element_type=F32)


def split_matrix():
    source, target = iota((256, 256), 0), iota((256, 256), 1)
    y = source % 32
    wanted = (y % 2) * 128 + source // 32 * 16 + y // 2
    return (target == wanted).astype(F32).astype(BF16)


def merge_matrix():
    source, target = iota((256, 256), 0), iota((256, 256), 1)
    y = target % 32
    wanted = (y % 2) * 128 + target // 32 * 16 + y // 2
    return (source == wanted).astype(F32).astype(BF16)


def pool_matrix():
    source, target = iota((256, 128), 0), iota((256, 128), 1)
    wanted = source // 32 * 16 + source % 16
    return (target == wanted).astype(F32).astype(BF16)


def spread_matrix():
    source, target = iota((128, 256), 0), iota((128, 256), 1)
    wanted = target // 32 * 16 + target % 16
    return (source == wanted).astype(F32).astype(BF16)


def even_cells(rows):
    shape = (rows, 128)
    return (iota(shape, 0) + iota(shape, 1) // 16) % 2 == 0


def swap(value, axis, offset):
    size = lax.axis_size(axis)
    pairs = []
    for i in range(offset, size - 1, 2):
        pairs += [(i, i + 1), (i + 1, i)]
    return lax.ppermute(value, axis, pairs)


def exchange(first, second, axis):
    return swap(first, axis, 0), swap(second, axis, 1)


def split_cells(cells, rows, packed, put):
    even = even_cells(4 * rows)
    both = exact_dot(cells, packed)
    first, second = both[:, :128], both[:, 128:]
    red = jnp.where(even, first, second)
    black = jnp.where(even, second, first)
    for m in range(4):
        put(m, 0, red[rows * m : rows * m + rows])
        put(m, 1, black[rows * m : rows * m + rows])


def pack_kernel(info, right, coef, packed):
    live = pl.program_id(0) < info[0]
    split = split_matrix()
    for half in range(2):
        lanes = slice(256 * half, 256 * half + 256)
        parts = [right[0, m, :, lanes] for m in range(3)] + [coef[0, :, lanes]]
        cells = jnp.where(live, jnp.concatenate(parts, axis=0), 0.0)

        def put(m, colour, value, half=half):
            packed[m, colour, half] = value

        split_cells(cells, 32, split, put)


def pack_rim_kernel(info, above, below, rim):
    held = info[0]
    split = split_matrix()
    for slot in range(SLOTS):
        for half in range(2):
            lanes = slice(256 * half, 256 * half + 256)
            parts = []
            for m in range(4):
                parts += [above[slot, m, :, lanes], below[slot, m, :, lanes]]
            cells = jnp.where(slot < held, jnp.concatenate(parts, axis=0), 0.0)

            def put(m, colour, value, tile=2 * slot + half):
                rim[m, colour, tile] = value

            split_cells(cells, 16, split, put)


def pack_edges_kernel(info, above, below, packed, edge_a, edge_b):
    held, odd = info[0], info[2] == 1
    parts, found = [], {}
    places = ((0, 0), (held - 1, 1))
    for m in range(4):
        for slot, half in places:
            lanes = slice(256 * half, 256 * half + 256)
            parts += [above[slot, m, :, lanes], below[slot, m, :, lanes]]

    def put(m, colour, value):
        found[m, colour] = value

    split_cells(jnp.concatenate(parts, axis=0), 32, split_matrix(), put)
    for slot, half in places:
        tile = 2 * slot + half
        for out, when in ((edge_a, odd), (edge_b, jnp.logical_not(odd))):

            @pl.when(when if half == 0 else jnp.logical_not(when))
            def _(out=out):
                for (m, colour), value in found.items():
                    out[m, colour, 0:8] = value[16 * half : 16 * half + 8]
                    out[m, colour, 8:40] = packed[m, colour, tile]
                    out[m, colour, 40:48] = value[16 * half + 8 : 16 * half + 16]


def load_fine(count, odd, factor, packed, rim, edge_a, edge_b, scaled, ratio, skip, rows):
    used = slice(skip, skip + rows)

    def put(tile, take):
        out = []
        for colour in range(2):
            coef = take(3, colour)
            inside = coef > 0.0
            for m in range(3):
                inverse = jnp.where(inside, 1.0 / (coef + 6.0 * factor[m]), 0.0)
                out.append((m, colour, take(m, colour) * inverse, factor[m] * inverse))
        for m, colour, first, second in out:
            scaled[m, colour, tile] = first
            ratio[m, colour, tile] = second

    def own(m, colour, tile):
        start, end = rim[m, colour, tile, skip:8], rim[m, colour, tile, 8 : 16 - skip]
        return jnp.concatenate([start, packed[m, colour, tile], end], axis=0)

    for tile in range(TILES):
        put(tile + 2, lambda m, colour: own(m, colour, tile))
    none = jnp.zeros((3, 2, rows, 128), F32)
    tile = WIDE - 2
    scaled[:, :, tile] = none
    ratio[:, :, tile] = none
    end = 2 * count + 2
    put(jnp.where(odd, 1, end), lambda m, colour: edge_a[m, colour, used])
    put(jnp.where(odd, end, 1), lambda m, colour: edge_b[m, colour, used])


def clear_rim(values, rows):
    rim = jnp.zeros((3, WIDE, 8, 128), F32)
    values[:, :, 0:8] = rim
    values[:, :, 8 + rows : 16 + rows] = rim
    side = jnp.zeros((3, rows, 128), F32)
    for tile in (0, WIDE - 1):
        values[:, tile, 8 : 8 + rows] = side


def fine_update(other, scaled, ratio, m, colour, tile, chunk, masks):
    lane_low, lane_high, even, edges = masks
    row = 8 + 8 * chunk
    here = other[m, tile, row : row + 8]
    total = here + other[m, tile, row - 1 : row + 7]
    total = total + other[m, tile, row + 1 : row + 9]
    before = other[m, tile - 1, row : row + 8]
    after = other[m, tile + 1, row : row + 8]
    total = total + pltpu.roll(jnp.where(lane_high, before, here), 16, 1)
    total = total + pltpu.roll(jnp.where(lane_low, after, here), 112, 1)
    up, down = pltpu.roll(here, 1, 1), pltpu.roll(here, 127, 1)
    beside = jnp.where(even, up, down) if colour == 0 else jnp.where(even, down, up)
    total = total + jnp.where(edges[colour], 0.0, beside)
    rows = slice(8 * chunk, 8 * chunk + 8)
    return scaled[m, colour, tile, rows] + ratio[m, colour, tile, rows] * total


def fine_masks():
    lane = iota((8, 128), 1)
    even = even_cells(8)
    first, last = lane % 16 == 0, lane % 16 == 15
    edges = (
        (even & first) | (jnp.logical_not(even) & last),
        (even & last) | (jnp.logical_not(even) & first),
    )
    return lane < 16, lane >= 112, even, edges


def fine_sweep(values, scaled, ratio, colour, masks, chunks, tiles=range(1, WIDE - 1)):
    for tile in tiles:
        for m in range(3):
            for chunk in chunks:
                values[colour][m, tile, 8 + 8 * chunk : 16 + 8 * chunk] = fine_update(
                    values[1 - colour], scaled, ratio, m, colour, tile, chunk, masks
                )


def down_kernel(
    info, factor, packed, rim, edge_a, edge_b, red, black, coarse, layers_a, layers_b, remain,
    scaled, ratio
):
    held, odd, odd_slab = info[0], info[2] == 1, info[3] == 1
    load_fine(held, odd, factor, packed, rim, edge_a, edge_b, scaled, ratio, 0, ROWS)
    masks = fine_masks()
    pre = (red, black)
    clear_rim(red, ROWS)
    clear_rim(black, ROWS)
    chunks = range(ROWS // 8)
    red[:, 1 : WIDE - 1, 8 : 8 + ROWS] = scaled[:, 0, 1 : WIDE - 1]
    fine_sweep(pre, scaled, ratio, 1, masks, chunks)
    fine_sweep(pre, scaled, ratio, 0, masks, chunks)
    fine_sweep(pre, scaled, ratio, 1, masks, chunks)

    for tile in range(2, 2 + TILES):
        for chunk in range(1, 5):
            row = 8 + 8 * chunk
            out = slice(8 * chunk - 8, 8 * chunk)
            coef = packed[3, 0, tile - 2, out]
            for m in range(3):
                reds = red[m, tile, row : row + 8]
                update = fine_update(black, scaled, ratio, m, 0, tile, chunk, masks)
                left = (coef + 6.0 * factor[m]) * (update - reds)
                remain[m, tile - 2, out] = jnp.where(tile < 2 * held + 2, left, 0.0)
            remain[3, tile - 2, out] = coef + packed[3, 1, tile - 2, out]
    sides = []
    for half in range(2):
        parts = []
        for tile in range(half, TILES, 2):
            for m in range(4):
                first = remain[m, tile, pl.ds(0, COWN, stride=2)]
                parts.append(first + remain[m, tile, pl.ds(1, COWN, stride=2)])
        sides.append(jnp.concatenate(parts, axis=0))
    pooled = exact_dot(jnp.concatenate(sides, axis=1), pool_matrix()) * 0.125
    for slot in range(SLOTS):
        for m in range(4):
            place = COWN * (4 * slot + m)
            box = pooled[place : place + COWN]
            coarse[m, slot] = box
            start, end = box[:CHALO], box[COWN - CHALO :]
            rows = slice(CHALO * slot, CHALO * slot + CHALO)
            layers_a[m, rows] = jnp.where(odd_slab, start, end)
            layers_b[m, rows] = jnp.where(odd_slab, end, start)


def keep_kernel(packed, red, black, remain, pre_red, pre_black, partial):
    skip = (ROWS - NARROW) // 2
    pre_red[...] = red[:, 1 : WIDE - 1, 8 + skip : 8 + skip + NARROW]
    pre_black[...] = black[:, 1 : WIDE - 1, 8 + skip : 8 + skip + NARROW]
    totals = [jnp.zeros((8, 128), F32) for _ in range(6)]
    for tile in range(TILES):
        for chunk in range(4):
            rows, inner = slice(8 * chunk, 8 * chunk + 8), slice(16 + 8 * chunk, 24 + 8 * chunk)
            for m in range(3):
                both = packed[m, 0, tile, rows] + remain[m, tile, rows]
                totals[m] = totals[m] + both * red[m, tile + 2, inner]
                totals[m + 3] = totals[m + 3] + packed[m, 1, tile, rows] * black[m, tile + 2, inner]
    partial[...] = sum(totals[1:], totals[0])


def edges_kernel(info, coarse, layers_a, layers_b, kept_red, kept_black, edge_a, edge_b, tall):
    held, odd, odd_slab = info[0], info[2] == 1, info[3] == 1

    group = iota((8, 128), 1) // 16

    def fill(out, slot, beside, first):
        for m in range(4):
            for n, source in enumerate((slot, beside)):
                rows = slice(CHALO * source, CHALO * source + CHALO)
                one, other = layers_a[m, rows], layers_b[m, rows]
                target = out if n == 0 else tall
                target[m, 0:CHALO] = jnp.where(odd_slab, one, other)
                target[m, CHALO : CHALO + COWN] = coarse[m, source]
                target[m, CHALO + COWN : CROWS] = jnp.where(odd_slab, other, one)
            extra = jnp.zeros((8, 128), F32)
            out[m, CROWS:40] = extra[: 40 - CROWS]
            for j, row in enumerate(EXTRA_ROWS):
                turn = 16 * j if first else 16 * (j + 1)
                piece = pltpu.roll(tall[m, row : row + 8], turn, 1)
                extra = jnp.where(group == j, piece, extra)
            out[m, 40:48] = extra

    for is_odd in (False, True):
        for count in range(2, SLOTS + 1):

            @pl.when((odd == is_odd) & (held == count))
            def _(is_odd=is_odd, count=count):
                start, end = (0, 1, True), (count - 1, count - 2, False)
                fill(edge_a, *(start if is_odd else end))
                fill(edge_b, *(end if is_odd else start))


def solve_kernel(
    info, factor, previous, coarse, layers_a, layers_b, coarse_a, coarse_b, partial, kept_red,
    kept_black, wanted, share, cscaled, cratio, cred, cblack
):
    held, odd, odd_slab = info[0], info[2] == 1, info[3] == 1

    def put(tile, row, pieces):
        coef = pieces[3]
        size = coef.shape[0]
        for m in range(3):
            b = 0.25 * factor[m]
            inverse = jnp.where(coef > 0.0, 1.0 / (coef + 6.0 * b), 0.0)
            cscaled[m, tile, row : row + size] = pieces[m] * inverse
            cratio[m, tile, row : row + size] = b * inverse

    rest = jnp.zeros((3, CWIDE, 40 - CROWS, 128), F32)
    cscaled[:, :, CROWS:] = rest
    cratio[:, :, CROWS:] = rest
    none = jnp.zeros((3, CROWS, 128), F32)
    for tile in (0, CWIDE - 3, CWIDE - 2, CWIDE - 1):
        cscaled[:, tile, :CROWS] = none
        cratio[:, tile, :CROWS] = none
    for slot in range(SLOTS):
        rows = slice(CHALO * slot, CHALO * slot + CHALO)
        ones = [layers_a[m, rows] for m in range(4)]
        others = [layers_b[m, rows] for m in range(4)]
        above = [jnp.where(odd_slab, ones[m], others[m]) for m in range(4)]
        below = [jnp.where(odd_slab, others[m], ones[m]) for m in range(4)]
        put(slot + 3, 0, above)
        put(slot + 3, CHALO, [coarse[m, slot] for m in range(4)])
        put(slot + 3, CHALO + COWN, below)
    lane = iota((8, 128), 1)
    for edge, is_left in ((coarse_a, odd), (coarse_b, jnp.logical_not(odd))):
        put(jnp.where(is_left, 2, held + 3), 0, [edge[m, 0:CROWS] for m in range(4)])
        tile = jnp.where(is_left, 1, held + 4)
        for j, row in enumerate(EXTRA_ROWS):
            pieces = []
            for m in range(4):
                extra = edge[m, 40:48]
                left = jnp.where(lane >= 112, pltpu.roll(extra, (112 - 16 * j) % 128, 1), 0.0)
                right = jnp.where(lane < 16, pltpu.roll(extra, (128 - 16 * j) % 128, 1), 0.0)
                pieces.append(jnp.where(is_left, left, right))
            put(tile, row, pieces)

    lane_low, lane_high = lane < 16, lane >= 112
    first, last = lane % 16 == 0, lane % 16 == 15
    is_red = (iota((8, 128), 0) + lane // 16 + lane % 16) % 2 == 0
    chosen = (is_red, jnp.logical_not(is_red))
    corr = (cred, cblack)
    rim = jnp.zeros((3, CWIDE, 8, 128), F32)
    side = jnp.zeros((3, 40, 128), F32)
    for value in corr:
        value[:, :, 0:8] = rim
        value[:, :, 48:56] = rim
    for tile in (0, CWIDE - 1):
        cred[:, tile, 8:48] = side
    for tile in (0, 1, CWIDE - 2, CWIDE - 1):
        cblack[:, tile, 8:48] = side
    for tile in range(1, CWIDE - 1):
        for m in range(3):
            for chunk in range(5):
                cred[m, tile, 8 + 8 * chunk : 16 + 8 * chunk] = jnp.where(
                    is_red, cscaled[m, tile, 8 * chunk : 8 * chunk + 8], 0.0
                )

    def coarse_sweep(colour, chunks):
        other = corr[1 - colour]
        for tile in range(2, CWIDE - 2):
            for m in range(3):
                for chunk in chunks:
                    row = 8 + 8 * chunk
                    here = other[m, tile, row : row + 8]
                    total = other[m, tile, row - 1 : row + 7] + other[m, tile, row + 1 : row + 9]
                    before = other[m, tile - 1, row : row + 8]
                    after = other[m, tile + 1, row : row + 8]
                    total = total + pltpu.roll(jnp.where(lane_high, before, here), 16, 1)
                    total = total + pltpu.roll(jnp.where(lane_low, after, here), 112, 1)
                    total = total + jnp.where(first, 0.0, pltpu.roll(here, 1, 1))
                    total = total + jnp.where(last, 0.0, pltpu.roll(here, 127, 1))
                    rows = slice(8 * chunk, 8 * chunk + 8)
                    new = cscaled[m, tile, rows] + cratio[m, tile, rows] * total
                    corr[colour][m, tile, row : row + 8] = jnp.where(chosen[colour], new, 0.0)

    for sweep, chunks in enumerate((5, 5, 4, 4, 4, 4)):
        coarse_sweep((sweep + 1) % 2, range(chunks))
    coarse_sweep(1, range(1, 4))

    total = partial[...]
    for slot in range(SLOTS):
        for m in range(3):
            for chunk in range(2):
                row = 8 + CHALO + 8 * chunk
                both = cred[m, slot + 3, row : row + 8] + cblack[m, slot + 3, row : row + 8]
                total = total + 8.0 * (coarse[m, slot, 8 * chunk : 8 * chunk + 8] * both)
    cells = jnp.full((1, 128), info[1], jnp.int32).astype(F32)
    cells = cells * (3.0 * lax.axis_size(SLAB_AXIS) * 32 * 512)
    part = jnp.sum(total, axis=0, keepdims=True) / cells / previous[0]
    share[...] = jnp.broadcast_to(part, share.shape)

    low = 8 + CHALO - 2
    for ctile in range(2, CWIDE - 2):
        for m in range(3):
            wanted[ctile - 2, NARROW // 2 * m : NARROW // 2 * (m + 1)] = (
                cred[m, ctile, low : low + NARROW // 2] + cblack[m, ctile, low : low + NARROW // 2]
            )


def up_kernel(
    info, factor, packed, rim, edge_a, edge_b, pre_red, pre_black, wanted, old, smoothed, carried,
    scaled, ratio, red, black, spread, filled, sem
):
    carry = pltpu.make_async_copy(old, carried, sem.at[SLOTS])
    carry.start()
    held, odd = info[0], info[2] == 1
    skip = (ROWS - NARROW) // 2
    load_fine(held, odd, factor, packed, rim, edge_a, edge_b, scaled, ratio, skip, NARROW)
    masks = fine_masks()
    values = (red, black)
    clear_rim(red, NARROW)
    clear_rim(black, NARROW)
    widen = spread_matrix()
    half_rows = NARROW // 2
    for ctile in range(2, CWIDE - 2):
        wide = exact_dot(wanted[ctile - 2], widen)
        for half in range(2):
            tile = 2 * (ctile - 3) + half + 2
            if not 1 <= tile <= WIDE - 2:
                continue
            for m in range(3):
                piece = wide[half_rows * m : half_rows * m + half_rows, 128 * half : 128 * half + 128]
                spread[m, tile, pl.ds(0, half_rows, stride=2)] = piece
                spread[m, tile, pl.ds(1, half_rows, stride=2)] = piece
    for value, old in ((red, pre_red), (black, pre_black)):
        for tile in range(1, WIDE - 1):
            for m in range(3):
                value[m, tile, 8 : 8 + NARROW] = old[m, tile - 1] + spread[m, tile]
    chunks = range(NARROW // 8)
    for _ in range(2):
        fine_sweep(values, scaled, ratio, 1, masks, chunks)
        fine_sweep(values, scaled, ratio, 0, masks, chunks)

    merge = merge_matrix()
    even = even_cells(3 * 32)
    own = slice(12, 44)
    copies = []
    for slot in range(SLOTS):
        live = slot < held
        for half in range(2):
            tile = 2 + 2 * slot + half
            reds = jnp.concatenate([red[m, tile, own] for m in range(3)], axis=0)
            blacks = jnp.concatenate([black[m, tile, own] for m in range(3)], axis=0)
            both = jnp.concatenate(
                [jnp.where(even, reds, blacks), jnp.where(even, blacks, reds)], axis=1
            )
            cells = exact_dot(jnp.where(live, both, 0.0), merge)
            for m in range(3):
                lanes = slice(256 * half, 256 * half + 256)
                filled[slot, m, :, lanes] = cells[32 * m : 32 * m + 32]
        copies.append(pltpu.make_async_copy(filled.at[slot], smoothed.at[slot], sem.at[slot]))
        copies[-1].start()
    for copy in copies + [carry]:
        copy.wait()


def add_kernel(shares, kept_red, kept_black, kept, total):
    total[...] = jnp.broadcast_to(jnp.sum(shares[...], axis=0, keepdims=True), total.shape)


def direction_kernel(
    info, shares, smoothed, old, same, direction, ready, ready_old, filled, sem
):
    held = info[0]
    fetches = []
    for slot in range(SLOTS):
        fetch = pltpu.make_async_copy(smoothed.at[slot], ready.at[slot], sem.at[slot])
        fetch_old = pltpu.make_async_copy(old.at[slot], ready_old.at[slot], sem.at[SLOTS + slot])
        fetch.start()
        fetch_old.start()
        fetches.append((fetch, fetch_old))
    ratio = jnp.sum(shares[...])
    copies = []
    for slot in range(SLOTS):
        for fetch in fetches[slot]:
            fetch.wait()
        filled[slot] = jnp.where(slot < held, ready[slot] + ratio * ready_old[slot], 0.0)
        target = direction.at[slot]
        copies.append(pltpu.make_async_copy(filled.at[slot], target, sem.at[2 * SLOTS + slot]))
        copies[-1].start()
    for copy in copies:
        copy.wait()


def shape(*dims):
    return jax.ShapeDtypeStruct(dims, F32)


SMEM = pl.BlockSpec(memory_space=pltpu.SMEM)
WHOLE = pl.BlockSpec(memory_space=pltpu.VMEM)
ANYWHERE = pl.BlockSpec(memory_space=pl.ANY)
IN_HBM = pl.BlockSpec(memory_space=pltpu.HBM)


def slot_block(*dims):
    return pl.BlockSpec((1,) + dims, lambda q: (q,) + (0,) * len(dims))


def per_device(box_counts, viscosity, implicit_coef, right_side, old_direction, previous_dot):
    group_n = lax.axis_size(GROUP_AXES)
    slab_n = lax.axis_size(SLAB_AXIS)
    right, coef = right_side[0], implicit_coef[0]
    params = pltpu.CompilerParams(vmem_limit_bytes=VMEM_BYTES)

    place = lax.axis_index(GROUP_AXES)
    info = jnp.stack(
        [
            lax.dynamic_index_in_dim(box_counts, place, 0, keepdims=False),
            jnp.sum(box_counts),
            place % 2,
            jnp.ones_like(place),
        ]
    ).astype(jnp.int32)

    top = jnp.concatenate([right[:, :, :8], coef[:, None, :8]], axis=1)
    bottom = jnp.concatenate([right[:, :, 24:], coef[:, None, 24:]], axis=1)
    above = lax.ppermute(bottom, SLAB_AXIS, [(i, i + 1) for i in range(slab_n - 1)])
    below = lax.ppermute(top, SLAB_AXIS, [(i + 1, i) for i in range(slab_n - 1)])

    packed = pl.pallas_call(
        pack_kernel,
        grid=(SLOTS,),
        in_specs=[SMEM, slot_block(3, 32, 512), slot_block(32, 512)],
        out_specs=pl.BlockSpec((4, 2, 2, 32, 128), lambda q: (0, 0, q, 0, 0)),
        out_shape=shape(4, 2, TILES, 32, 128),
        compiler_params=params,
        cost_estimate=pl.CostEstimate(flops=20000000, bytes_accessed=2000000, transcendentals=0),
        name="pack",
    )(info, right, coef)
    edges = pl.pallas_call(
        pack_edges_kernel,
        in_specs=[SMEM] + [WHOLE] * 3,
        out_specs=[WHOLE] * 2,
        out_shape=[shape(4, 2, ROWS, 128)] * 2,
        compiler_params=params,
        name="pack_edges",
    )(info, above, below, packed)
    edges = exchange(*edges, GROUP_AXES)
    rim = pl.pallas_call(
        pack_rim_kernel,
        in_specs=[SMEM] + [WHOLE] * 2,
        out_specs=WHOLE,
        out_shape=shape(4, 2, TILES, 16, 128),
        compiler_params=params,
        cost_estimate=pl.CostEstimate(flops=10000000, bytes_accessed=1000000, transcendentals=0),
        name="pack_rim",
    )(info, above, below)

    padded = shape(3, WIDE, ROWS + 16, 128)
    fine = pltpu.VMEM((3, 2, WIDE, ROWS, 128), F32)
    layer_shape = shape(4, SLOTS * CHALO, 128)
    red, black, coarse, *layers, remain = pl.pallas_call(
        down_kernel,
        in_specs=[SMEM] * 2 + [WHOLE] * 4,
        out_specs=[WHOLE] * 6,
        out_shape=[
            padded,
            padded,
            shape(4, SLOTS, COWN, 128),
            layer_shape,
            layer_shape,
            shape(4, TILES, 32, 128),
        ],
        scratch_shapes=[fine, fine],
        compiler_params=params,
        name="down",
    )(info, viscosity, packed, rim, *edges)

    start, end = layers
    layers = (
        lax.ppermute(end, SLAB_AXIS, [(i, i + 1) for i in range(slab_n - 1)]),
        lax.ppermute(start, SLAB_AXIS, [(i + 1, i) for i in range(slab_n - 1)]),
    )
    pre_red, pre_black, partial = pl.pallas_call(
        keep_kernel,
        in_specs=[WHOLE] * 4,
        out_specs=[WHOLE] * 3,
        out_shape=[shape(3, WIDE - 2, NARROW, 128)] * 2 + [shape(8, 128)],
        compiler_params=params,
        cost_estimate=pl.CostEstimate(flops=4000000, bytes_accessed=1000000, transcendentals=0),
        name="keep",
    )(packed, red, black, remain)
    coarse_edges = pl.pallas_call(
        edges_kernel,
        in_specs=[SMEM] + [WHOLE] * 5,
        out_specs=[WHOLE] * 2,
        out_shape=[shape(4, 48, 128)] * 2,
        scratch_shapes=[pltpu.VMEM((4, 40, 128), F32)],
        compiler_params=params,
        name="edges",
    )(info, coarse, *layers, pre_red, pre_black)
    coarse_edges = exchange(*coarse_edges, GROUP_AXES)

    narrow = pltpu.VMEM((3, 2, WIDE, NARROW, 128), F32)
    value = pltpu.VMEM((3, WIDE, NARROW + 16, 128), F32)
    cfine = pltpu.VMEM((3, CWIDE, 40, 128), F32)
    cvalue = pltpu.VMEM((3, CWIDE, 56, 128), F32)
    wanted, share = pl.pallas_call(
        solve_kernel,
        in_specs=[SMEM] * 3 + [WHOLE] * 8,
        out_specs=[WHOLE] * 2,
        out_shape=[shape(CWIDE - 4, 3 * NARROW // 2, 128), shape(group_n, 128)],
        scratch_shapes=[cfine, cfine, cvalue, cvalue],
        compiler_params=params,
        name="solve",
    )(info, viscosity, previous_dot, coarse, *layers, *coarse_edges, partial, pre_red, pre_black)

    whole = shape(SLOTS, 3, 32, 512)
    held_whole = pltpu.VMEM((SLOTS, 3, 32, 512), F32)
    smoothed, carried = pl.pallas_call(
        up_kernel,
        in_specs=[SMEM] * 2 + [WHOLE] * 7 + [ANYWHERE],
        out_specs=[IN_HBM] * 2,
        out_shape=[whole] * 2,
        scratch_shapes=[
            narrow,
            narrow,
            value,
            value,
            pltpu.VMEM((3, WIDE, NARROW, 128), F32),
            held_whole,
            pltpu.SemaphoreType.DMA((SLOTS + 1,)),
        ],
        compiler_params=params,
        cost_estimate=pl.CostEstimate(flops=40000000, bytes_accessed=8000000, transcendentals=0),
        name="up",
    )(
        info, viscosity, packed, rim, *edges, pre_red, pre_black, wanted, old_direction[0]
    )

    shares = lax.all_to_all(share, GROUP_AXES, 0, 0)
    shares = pl.pallas_call(
        add_kernel,
        in_specs=[WHOLE] * 4,
        out_specs=WHOLE,
        out_shape=shape(slab_n, 128),
        compiler_params=params,
        name="add",
    )(shares, pre_red, pre_black, wanted)
    shares = lax.all_to_all(shares, SLAB_AXIS, 0, 0)
    smoothed, direction = pl.pallas_call(
        direction_kernel,
        in_specs=[SMEM, WHOLE, IN_HBM, IN_HBM],
        out_specs=[IN_HBM] * 2,
        out_shape=[whole] * 2,
        input_output_aliases={2: 0, 3: 1},
        scratch_shapes=[held_whole] * 3 + [pltpu.SemaphoreType.DMA((3 * SLOTS,))],
        compiler_params=params,
        name="direction",
    )(info, shares, smoothed, carried)
    return smoothed[None], direction[None]


def solution(mesh):
    wide = P("gx", GROUP_AXES, None, None, None)
    placed = (P(), P(), P("gx", GROUP_AXES, None, None), wide, wide, P())
    return jax.shard_map(
        per_device, mesh=mesh, in_specs=placed, out_specs=(wide, wide), check_vma=False
    )
```
